256 devices in a mesh: group: 2 (over z_hi), rows: 8 (over z_lo, core), dp: 16 (over x, y).
Axes of the slice: x: 4, y: 4, z: 8 (z_hi: 2, z_lo: 4; z = z_hi * 4 + z_lo), core: 2. Of those that a mesh axis runs over, the one named last changes fastest.
Arguments:
- teacher_tokens: bfloat16 [65536, 1536], P(('rows', 'dp')), may hold values from -40 to 40
- teacher_qkv: bfloat16 [1536, 4608], P('rows'), may hold values from -20 to 20
- teacher_out: bfloat16 [1536, 1536], P('rows'), may hold values from -0.15625 to 0.15625
- student_tokens: bfloat16 [65536, 1024], P(('rows', 'dp')), may hold values from -40 to 40
- student_weights: bfloat16 [1024, 4096], P('rows'), may hold values from -20 to 20
Outputs:
- student_grad: float32 [1024, 4096], P(('group', 'rows'), 'dp')
The draws below stay inside these ranges and needn't reach their ends.
All inputs are finite; a program needn't handle non-finite values.
Results may differ from the reference program's by a relative error of at most 0.009.
Values may be sent and summed in bfloat16 or wider, within the bound.
A program may use at most 128 MiB of HBM per device.

```python
import math
import jax
import jax.numpy as jnp
from jax import lax

D_T = 1536
D_S = 1024
HEAD = 64
IMG_TOK = 256
TOK_DEV = 512
IMAGES = 256
TOKENS = 65536
N_ROWS = 8
N_DP = 16


def feature_scales(key, row_count, model_width):
    key_col, key_row = jax.random.split(key)
    low = math.log(0.3)
    high = math.log(3.0)
    column_scale = jnp.exp(jax.random.uniform(key_col, (1, model_width), minval=low, maxval=high))
    row_scale = jnp.exp(jax.random.uniform(key_row, (row_count, 1), minval=low, maxval=high))
    return column_scale * row_scale


def draw_teacher_tokens(key, part):
    key = jax.random.fold_in(key, 21)
    key_scale, key_base = jax.random.split(key, 2)
    scales = feature_scales(key_scale, TOKENS, D_T)
    field = jnp.clip(jax.random.normal(key_base, (TOKENS, D_T)), -4.0, 4.0) * scales
    return field.astype(jnp.bfloat16)


def draw_student_tokens(key, part):
    key = jax.random.fold_in(key, 22)
    key_scale, key_base = jax.random.split(key, 2)
    scales = feature_scales(key_scale, TOKENS, D_S)
    field = jnp.clip(jax.random.normal(key_base, (TOKENS, D_S)), -4.0, 4.0) * scales
    return field.astype(jnp.bfloat16)


def draw_teacher_qkv(key, part):
    key = jax.random.fold_in(key, 23)
    matrix = jnp.clip(jax.random.normal(key, (D_T, 3 * D_T)), -4.0, 4.0) / math.sqrt(D_T)
    return matrix.astype(jnp.bfloat16)


def draw_student_weights(key, part):
    key = jax.random.fold_in(key, 24)
    matrix = jnp.clip(jax.random.normal(key, (D_S, 4 * D_S)), -4.0, 4.0) / math.sqrt(D_S)
    return matrix.astype(jnp.bfloat16)


def block_levels(rng, extent, cuts, smallest, largest):
    def one(position, parts):
        steps = jax.random.uniform(jax.random.fold_in(jax.random.fold_in(rng, 6), position), (parts,), jnp.float32, smallest / len(cuts), largest / len(cuts))
        return jnp.repeat(jnp.exp(steps), extent[position] // parts).reshape((-1,) + (1,) * (len(extent) - position - 1))

    factor_of = one(*cuts[0])
    for cut in cuts[1:]:
        factor_of = factor_of * one(*cut)
    return factor_of


def gaussian(key, shape, width, most, shards=(), kind=jnp.bfloat16):
    level = block_levels(key, shape, shards, -0.22, 0.18) if shards else 1.0
    entries = jax.random.normal(key, shape, jnp.float32) * width * level
    return jnp.minimum(jnp.maximum(entries, -most), most).astype(kind)


def setup_inputs(seed: int = 0) -> dict:
    streams_of = jax.random.split(jax.random.key(seed), 6)
    return {
        "teacher_tokens": draw_teacher_tokens(jax.random.fold_in(streams_of[5], 71), 0),
        "teacher_qkv": draw_teacher_qkv(jax.random.fold_in(streams_of[5], 71), 0),
        "teacher_out": gaussian(streams_of[2], (D_T, D_T), D_T ** -0.5, 0.15625, ((0, 8),)),
        "student_tokens": draw_student_tokens(jax.random.fold_in(streams_of[5], 71), 0),
        "student_weights": draw_student_weights(jax.random.fold_in(streams_of[5], 71), 0),
    }


epsilon = 1e-06
distill_weight = 512.0

def normed(tokens):
    values = tokens.astype(jnp.float32)
    centred = values - lax.optimization_barrier(jnp.mean(values, axis=-1, keepdims=True))
    spread = lax.optimization_barrier(jnp.mean(centred * centred, axis=-1, keepdims=True))
    return (centred * lax.rsqrt(spread + epsilon)).astype(jnp.bfloat16)

def attention_fwd(qkv_act, model_width, head_size):
    images = qkv_act.shape[0] // IMG_TOK
    head_count = model_width // head_size
    shaped = qkv_act.astype(jnp.float32).reshape(images, IMG_TOK, 3, head_count, head_size)
    queries = shaped[:, :, 0]
    keys_f = shaped[:, :, 1]
    values_f = shaped[:, :, 2]
    scores = jnp.einsum('bihe,bjhe->bhij', queries, keys_f) * head_size ** (-0.5)
    scores = scores - lax.optimization_barrier(jnp.max(scores, axis=-1, keepdims=True))
    exps_raw = jnp.exp(scores)
    softmax_out = exps_raw / lax.optimization_barrier(jnp.sum(exps_raw, axis=-1, keepdims=True))
    probs_b = softmax_out.astype(jnp.bfloat16)
    mixed_out = jnp.einsum('bhij,bjhe->bihe', probs_b.astype(jnp.float32), values_f)
    return (mixed_out.reshape(qkv_act.shape[0], model_width).astype(jnp.bfloat16), softmax_out, probs_b)

def attention_bwd(qkv_act, softmax_out, probs_b, mixed_grad, model_width, head_size):
    images = qkv_act.shape[0] // IMG_TOK
    head_count = model_width // head_size
    shaped = qkv_act.astype(jnp.float32).reshape(images, IMG_TOK, 3, head_count, head_size)
    queries = shaped[:, :, 0]
    keys_f = shaped[:, :, 1]
    values_f = shaped[:, :, 2]
    upstream = mixed_grad.astype(jnp.float32).reshape(images, IMG_TOK, head_count, head_size)
    prob_grad = jnp.einsum('bihe,bjhe->bhij', upstream, values_f)
    value_grad = jnp.einsum('bhij,bihe->bjhe', probs_b.astype(jnp.float32), upstream).astype(jnp.bfloat16)
    row_total = lax.optimization_barrier(jnp.sum(prob_grad * softmax_out, axis=-1, keepdims=True))
    score_grad = (softmax_out * (prob_grad - row_total) * head_size ** (-0.5)).astype(jnp.bfloat16)
    score_f = score_grad.astype(jnp.float32)
    query_grad = jnp.einsum('bhij,bjhe->bihe', score_f, keys_f).astype(jnp.bfloat16)
    key_grad = jnp.einsum('bhij,bihe->bjhe', score_f, queries).astype(jnp.bfloat16)
    stacked = jnp.stack([query_grad, key_grad, value_grad], axis=2)
    return stacked.reshape(qkv_act.shape[0], 3 * model_width)

def gram_of(features):
    model_width = features.shape[1]
    row_scale = lax.rsqrt(lax.optimization_barrier(jnp.mean(features * features, axis=-1, keepdims=True)) + epsilon) * model_width ** (-0.5)
    unit_rows = (features * row_scale).reshape(-1, IMG_TOK, model_width)
    return jnp.einsum('bic,bjc->bij', unit_rows, unit_rows, precision=lax.Precision.HIGHEST)

def output_grad(student_result, teacher_gram, weight):

    def loss_of(result_rows):
        difference = gram_of(result_rows) - teacher_gram
        return weight * jnp.sum(difference * difference)
    primal, pullback = jax.vjp(loss_of, student_result)
    return pullback(jnp.ones_like(primal))[0].astype(jnp.bfloat16)

def reference(teacher_tokens, teacher_qkv, teacher_out, student_tokens, student_weights):
    blocks = N_ROWS * N_DP
    teacher_blocks = teacher_tokens.reshape(blocks, TOK_DEV, D_T)
    student_blocks = student_tokens.reshape(blocks, TOK_DEV, D_S)
    weight = distill_weight / IMAGES
    w_qkv = student_weights[:, :3 * D_S]
    w_out = student_weights[:, 3 * D_S:]

    def step(running, pair):
        tokens_t, tokens_s = pair
        normed_t = normed(tokens_t)
        act_t = jnp.dot(normed_t, teacher_qkv, preferred_element_type=jnp.float32).astype(jnp.bfloat16)
        mixed_t, unused_probs, unused_b = attention_fwd(act_t, D_T, HEAD)
        features_t = (tokens_t.astype(jnp.float32) + jnp.dot(mixed_t, teacher_out, preferred_element_type=jnp.float32)).astype(jnp.bfloat16)
        teacher_gram = gram_of(features_t.astype(jnp.float32))
        normed_s = normed(tokens_s)
        act_s = jnp.dot(normed_s, w_qkv, preferred_element_type=jnp.float32).astype(jnp.bfloat16)
        mixed_s, softmax_out, probs_b = attention_fwd(act_s, D_S, HEAD)
        result_s = tokens_s.astype(jnp.float32) + jnp.dot(mixed_s, w_out, preferred_element_type=jnp.float32)
        out_grad = output_grad(result_s, teacher_gram, weight)
        mixed_grad = jnp.dot(out_grad, w_out.T, preferred_element_type=jnp.float32).astype(jnp.bfloat16)
        act_grad = attention_bwd(act_s, softmax_out, probs_b, mixed_grad, D_S, HEAD)
        grad_in = jnp.dot(normed_s.T, act_grad, preferred_element_type=jnp.float32)
        grad_out = jnp.dot(mixed_s.T, out_grad, preferred_element_type=jnp.float32)
        return (running + jnp.concatenate([grad_in, grad_out], axis=1), None)
    total, unused = lax.scan(step, jnp.zeros((D_S, 4 * D_S), jnp.float32), (teacher_blocks, student_blocks))
    return total
```

```python
import jax
import jax.numpy as jnp
from jax import lax
from jax.experimental import pallas as pl
from jax.experimental.pallas import tpu as pltpu
from jax.sharding import PartitionSpec as P

MESH = pl.DeviceIdType.MESH
BF = jnp.bfloat16
F32 = jnp.float32

T = 256
DT = 1536
DS = 1024
TW = 4 * DT
SW = 4 * DS
RT = DT // 8
RS = DS // 8
QT = RT // 4
QS = RS // 4
EPS = 1e-06
EXP2_SCALE = 0.125 * 1.4426950408889634

CHUNKS = (
    [(True, 768 * i, 768) for i in range(6)]
    + [(False, 1024 * i, 1024) for i in range(3)]
    + [(True, 4608 + 768 * i, 768) for i in range(2)]
    + [(False, 3072, 1024)]
)
NC = len(CHUNKS)


def mm(a, b, ca=1, cb=0):
    return lax.dot_general(a, b, (((ca,), (cb,)), ((), ())), preferred_element_type=F32)


def kernel(
    tt, tq, to, st, sw, out,
    Wt, Ws, xt, xs, nt, ns, at, mt, as_, pr, ms, gt, tr, lt, rg, mg,
    gp, l1, r1, l2, r2, gp2, bl1, br1, bl2, br2, z3, zr,
    loc_sem, zs_send, zs_recv, a_send, al_recv, ar_recv, b_send, bl_recv, br_recv, c_send, c_recv,
    x_send, x_recv, p1_send, pl1_recv, pr1_recv, pl2_recv, pr2_recv,
    p2_send, ql1_recv, qr1_recv, ql2_recv, qr2_recv, p3_send, p3_recv,
):
    g = lax.axis_index("group")
    r = lax.axis_index("rows")
    d = lax.axis_index("dp")
    zl, c = lax.div(r, 2), lax.rem(r, 2)
    z = g * 4 + zl
    x, y = lax.div(d, 4), lax.rem(d, 4)
    oc = 1 - c
    ma = x * oc + y * c
    mb = y * oc + x * c

    def a_peer(step):
        return {"dp": 4 * lax.rem(x + step * oc, 4) + lax.rem(y + step * c, 4)}

    def b_peer(step):
        return {"dp": 4 * lax.rem(x + step * c, 4) + lax.rem(y + step * oc, 4)}

    def z_peer(step):
        far = lax.rem(z + step, 8)
        return {"group": lax.div(far, 4), "rows": 2 * lax.rem(far, 4) + c}

    sibling = {"rows": r + 1 - 2 * c}

    def send(src, dst, send_sem, recv_sem, to_whom):
        pltpu.make_async_remote_copy(
            src_ref=src, dst_ref=dst, send_sem=send_sem, recv_sem=recv_sem,
            device_id=to_whom, device_id_type=MESH,
        ).start()

    def wait(ref, sem):
        pltpu.make_async_copy(ref, ref, sem).wait()

    local = [
        pltpu.make_async_copy(tt.at[pl.ds(g * T, T)], xt, loc_sem.at[0]),
        pltpu.make_async_copy(st.at[pl.ds(g * T, T)], xs, loc_sem.at[1]),
        pltpu.make_async_copy(tq, Wt.at[zl, c, :, 0:4608], loc_sem.at[2]),
        pltpu.make_async_copy(to, Wt.at[zl, c, :, 4608:6144], loc_sem.at[3]),
        pltpu.make_async_copy(sw, Ws.at[zl, c], loc_sem.at[4]),
    ]
    for copy in local:
        copy.start()

    barrier = pltpu.get_barrier_semaphore()
    peers = [z_peer(s) for s in range(1, 8)] + [a_peer(1), a_peer(3), b_peer(1), b_peer(3), sibling]
    for peer in peers:
        pl.semaphore_signal(barrier, inc=1, device_id=peer, device_id_type=MESH)
    pl.semaphore_wait(barrier, len(peers))

    def piece(chunk, shard, quarter, cols):
        teacher = CHUNKS[chunk][0]
        size = QT if teacher else QS
        rows = pl.ds(pl.multiple_of(quarter * size, 16), size)
        return (Wt if teacher else Ws).at[shard, c, rows, cols]

    def whole(chunk):
        _, first, count = CHUNKS[chunk]
        return slice(first, first + count)

    def half(chunk, which):
        _, first, count = CHUNKS[chunk]
        return slice(first + which * count // 2, first + (which + 1) * count // 2)

    def three(chunk, cols):
        teacher = CHUNKS[chunk][0]
        return (Wt.at[0, 0, 0 : 3 * QT, cols]) if teacher else (Ws.at[0, 0, 0 : 3 * QS, cols])

    def six(chunk, cols):
        teacher = CHUNKS[chunk][0]
        return (Wt.at[0, :, 0 : 3 * QT, cols]) if teacher else (Ws.at[0, :, 0 : 3 * QS, cols])

    def core_half(chunk, core):
        teacher = CHUNKS[chunk][0]
        return (Wt if teacher else Ws).at[:, core, :, whole(chunk)]

    for k in range(NC):
        teacher, first, count = CHUNKS[k]
        size = QT if teacher else QS
        rows = pl.ds(pl.multiple_of(ma * size, 16), size)
        if not teacher:
            src = sw.at[rows, whole(k)]
        elif first < 4608:
            src = tq.at[rows, whole(k)]
        else:
            src = to.at[rows, slice(first - 4608, first - 4608 + count)]
        for step in (1, 7, 2 if k % 2 == 0 else 6):
            send(src, piece(k, zl, ma, whole(k)), zs_send.at[k], zs_recv.at[k], z_peer(step))

    def stage_a(k):
        wait(three(k, whole(k)), zs_recv.at[k])
        for j in (1, 2, 3):
            src = piece(k, lax.rem(zl + j, 4), ma, whole(k))
            send(src, src, a_send.at[k], al_recv.at[k], a_peer(1))
            send(src, src, a_send.at[k], ar_recv.at[k], a_peer(3))

    def stage_b(k):
        wait(three(k, whole(k)), al_recv.at[k])
        for j in (1, 2, 3):
            src = piece(k, lax.rem(zl + j, 4), lax.rem(ma + 3, 4), half(k, 0))
            send(src, src, b_send.at[k], bl_recv.at[k], a_peer(1))
        wait(three(k, whole(k)), ar_recv.at[k])
        for j in (1, 2, 3):
            src = piece(k, lax.rem(zl + j, 4), lax.rem(ma + 1, 4), half(k, 1))
            send(src, src, b_send.at[k], br_recv.at[k], a_peer(3))

    def stage_c(k):
        wait(three(k, half(k, 0)), bl_recv.at[k])
        wait(three(k, half(k, 1)), br_recv.at[k])
        send(core_half(k, c), core_half(k, c), c_send.at[k], c_recv.at[k], sibling)

    def stage_d(k):
        wait(core_half(k, 0), c_recv.at[k])

    progress = [0]

    def pump(upto):
        while progress[0] < upto:
            t = progress[0]
            if t < NC:
                stage_a(t)
            if 0 <= t - 1 < NC:
                stage_b(t - 1)
            if 0 <= t - 2 < NC:
                stage_c(t - 2)
            progress[0] = t + 1

    def ready(k):
        pump(min(k + 4, NC + 2))
        stage_d(k)

    def norm(v):
        v = v.astype(F32)
        v = v - jnp.mean(v, axis=-1, keepdims=True)
        s = jnp.mean(v * v, axis=-1, keepdims=True)
        return v * lax.rsqrt(s + EPS)

    for copy in local:
        copy.wait()
    nt[...] = norm(xt[...]).astype(BF)

    def share_left(which, value):
        tr[which] = value.T.astype(BF).reshape(8, 2, 64, T)
        cols = pl.ds(pl.multiple_of(c * T, T), T)
        send(tr.at[which, :, oc], lt.at[which, :, :, cols], x_send.at[which], x_recv.at[which], sibling)
        lt[which, :, :, cols] = tr[which, :, c]

    normed_s = norm(xs[...])
    ns[...] = normed_s.astype(BF)
    share_left(0, normed_s)
    pump(2)

    lane = lax.broadcasted_iota(jnp.int32, (1, 128), 1)
    low_f = jnp.where(lane < 64, 1.0, 0.0).astype(F32)
    high_f = 1.0 - low_f
    low_b, high_b = low_f.astype(BF), high_f.astype(BF)

    def softmax_parts(q, k):
        s = mm(q, k, 1, 1) * EXP2_SCALE
        e = jnp.exp2(s - jnp.max(s, axis=-1, keepdims=True))
        return e, 1.0 / jnp.sum(e, axis=-1, keepdims=True)

    def lanes(start):
        return pl.ds(pl.multiple_of(start, 128), 128)

    def teacher_pair(h, carry):
        q, k, v = at[:, lanes(h * 128)], at[:, lanes(DT + h * 128)], at[:, lanes(2 * DT + h * 128)]
        e0, i0 = softmax_parts(q * low_b, k)
        o0 = mm(e0.astype(BF), v) * i0
        e1, i1 = softmax_parts(q * high_b, k)
        o1 = mm(e1.astype(BF), v) * i1
        mt[:, lanes(h * 128)] = (o0 * low_f + o1 * high_f).astype(BF)
        return carry

    def student_pair(h, carry):
        q, k, v = as_[:, lanes(h * 128)], as_[:, lanes(DS + h * 128)], as_[:, lanes(2 * DS + h * 128)]
        e0, i0 = softmax_parts(q * low_b, k)
        p0 = (e0 * i0).astype(BF)
        pr[2 * h] = p0
        o0 = mm(p0, v)
        e1, i1 = softmax_parts(q * high_b, k)
        p1 = (e1 * i1).astype(BF)
        pr[2 * h + 1] = p1
        o1 = mm(p1, v)
        ms[:, lanes(h * 128)] = (o0 * low_f + o1 * high_f).astype(BF)
        return carry

    def weights(k, first, count):
        if CHUNKS[k][0]:
            return Wt[:, :, :, first : first + count].reshape(DT, count)
        return Ws[:, :, :, first : first + count].reshape(DS, count)

    for k in range(6):
        ready(k)
        _, first, count = CHUNKS[k]
        for n in range(first, first + count, 256):
            at[:, n : n + 256] = mm(nt[...], weights(k, n, 256)).astype(BF)
    for part in range(3):
        lax.fori_loop(4 * part, 4 * part + 4, teacher_pair, 0)
        pump(min(progress[0] + 1, NC + 2))
    for k in range(6, 9):
        ready(k)
        _, first, count = CHUNKS[k]
        for n in range(first, first + count, 256):
            as_[:, n : n + 256] = mm(ns[...], weights(k, n, 256)).astype(BF)
    for part in range(2):
        lax.fori_loop(4 * part, 4 * part + 4, student_pair, 0)
        pump(min(progress[0] + 1, NC + 2))
    share_left(1, ms[...].astype(F32))

    for k in (9, 10):
        ready(k)
        _, first, count = CHUNKS[k]
        for n in range(first, first + count, 256):
            cols = slice(n - 4608, n - 4608 + 256)
            xt[:, cols] = (xt[:, cols].astype(F32) + mm(mt[...], weights(k, n, 256))).astype(BF)
    feats = xt[...].astype(F32)
    row = lax.rsqrt(jnp.mean(feats * feats, axis=-1, keepdims=True) + EPS) * DT**-0.5
    along = jnp.broadcast_to(row, (T, 128)).T[0:1, :]
    gt[...] = mm(xt[...], xt[...], 1, 1) * row * along

    ready(11)
    res = xs[...].astype(F32) + mm(ms[...], weights(11, 3072, 1024))
    scale = lax.rsqrt(jnp.mean(res * res, axis=-1, keepdims=True) + EPS) * DS**-0.5
    unit = res * scale
    uh = unit.astype(BF)
    ul = (unit - uh.astype(F32)).astype(BF)
    diff = mm(uh, uh, 1, 1) + (mm(uh, ul, 1, 1) + mm(ul, uh, 1, 1)) - gt[...]
    eh = diff.astype(BF)
    el = (diff - eh.astype(F32)).astype(BF)
    du = 8.0 * (mm(eh, uh) + (mm(eh, ul) + mm(el, uh)))
    og = (scale * (du - jnp.sum(du * unit, axis=-1, keepdims=True) * unit)).astype(BF)
    rg[c, :, 3072:4096] = og
    own_out = rg.at[c, :, 3072:4096]
    send(own_out, own_out, x_send.at[2], x_recv.at[2], sibling)
    for s in range(4):
        for core in range(2):
            mg[:, s * 256 + core * 128 : s * 256 + core * 128 + 128] = mm(
                og, Ws[s, core, :, 3072:4096], 1, 1
            ).astype(BF)

    def backward_pair(h, carry):
        q, k, v = as_[:, lanes(h * 128)], as_[:, lanes(DS + h * 128)], as_[:, lanes(2 * DS + h * 128)]
        up = mg[:, lanes(h * 128)]
        parts = []
        for e, mask in ((0, low_b), (1, high_b)):
            p = pr[2 * h + e]
            pf = p.astype(F32)
            dp = mm(up * mask, v, 1, 1)
            total = jnp.sum(dp * pf, axis=-1, keepdims=True)
            sg = (pf * (dp - total) * 0.125).astype(BF)
            parts.append((mm(sg, k), mm(sg, q, 0, 0), mm(p, up, 0, 0)))
        for i in range(3):
            joined = parts[0][i] * low_f + parts[1][i] * high_f
            rg[c, :, lanes(i * DS + h * 128)] = joined.astype(BF)
        return carry

    lax.fori_loop(0, 8, backward_pair, 0)
    own_in = rg.at[c, :, 0:3072]
    send(own_in, own_in, x_send.at[3], x_recv.at[3], sibling)
    wait(lt.at[0, :, :, 0:T], x_recv.at[0])
    wait(lt.at[1, :, :, 0:T], x_recv.at[1])
    wait(rg.at[0, :, 3072:4096], x_recv.at[2])
    wait(rg.at[0, :, 0:3072], x_recv.at[3])

    def block(a, i):
        return (4 * a + i) * oc + (4 * i + a) * c

    def make(a, i):
        n = block(a, i)
        left = lt[lax.div(n, 12)].reshape(512, 512)
        right = rg[:, :, pl.ds(pl.multiple_of(n * 256, 256), 256)].reshape(512, 256)
        gp[n] = mm(left, right).astype(BF)
        return n

    far, right_a, left_a = lax.rem(ma + 2, 4), lax.rem(ma + 1, 4), lax.rem(ma + 3, 4)

    def far_step(i, carry):
        n = make(far, i)
        send(gp.at[n], l1.at[i], p1_send.at[0, i], pl1_recv.at[i], a_peer(1))
        m = make(far, i + 2)
        send(gp.at[m], r1.at[i], p1_send.at[1, i], pr1_recv.at[i], a_peer(3))
        return carry

    lax.fori_loop(0, 2, far_step, 0)

    def near_step(i, carry):
        n = make(right_a, i + 2)
        send(gp.at[n], l2.at[i + 2], p1_send.at[2, i], pl2_recv.at[i + 2], a_peer(1))
        m = make(left_a, i)
        send(gp.at[m], r2.at[i], p1_send.at[3, i], pr2_recv.at[i], a_peer(3))
        return carry

    lax.fori_loop(0, 2, near_step, 0)

    def sum_make(i, carry):
        make(right_a, i)
        make(left_a, i + 2)
        return carry

    lax.fori_loop(0, 2, sum_make, 0)

    def own_make(i, carry):
        make(ma, i)
        return carry

    lax.fori_loop(0, 4, own_make, 0)

    def sum_step(i, carry):
        n = block(right_a, i)
        wait(l1.at[0], pl1_recv.at[i])
        gp[n] = (gp[n].astype(F32) + l1[i].astype(F32)).astype(BF)
        send(gp.at[n], l2.at[i], p1_send.at[4, i], pl2_recv.at[i], a_peer(1))
        m = block(left_a, i + 2)
        wait(r1.at[0], pr1_recv.at[i])
        gp[m] = (gp[m].astype(F32) + r1[i].astype(F32)).astype(BF)
        send(gp.at[m], r2.at[i + 2], p1_send.at[5, i], pr2_recv.at[i + 2], a_peer(3))
        return carry

    lax.fori_loop(0, 2, sum_step, 0)

    def close(i):
        n = block(ma, i)
        wait(l2.at[0], pl2_recv.at[i])
        wait(r2.at[0], pr2_recv.at[i])
        gp2[i] = (gp[n].astype(F32) + (l2[i].astype(F32) + r2[i].astype(F32))).astype(BF)

    far_b, right_b, left_b = lax.rem(mb + 2, 4), lax.rem(mb + 1, 4), lax.rem(mb + 3, 4)
    upper, lower = slice(0, 256), slice(256, 512)
    close(far_b)
    send(gp2.at[far_b, upper], bl1, p2_send.at[0], ql1_recv, b_peer(1))
    send(gp2.at[far_b, lower], br1, p2_send.at[1], qr1_recv, b_peer(3))
    close(right_b)
    send(gp2.at[right_b, lower], bl2.at[lower], p2_send.at[2], ql2_recv.at[1], b_peer(1))
    close(left_b)
    send(gp2.at[left_b, upper], br2.at[upper], p2_send.at[3], qr2_recv.at[0], b_peer(3))
    close(mb)
    wait(bl1, ql1_recv)
    gp2[right_b, upper] = (gp2[right_b, upper].astype(F32) + bl1[...].astype(F32)).astype(BF)
    send(gp2.at[right_b, upper], bl2.at[upper], p2_send.at[4], ql2_recv.at[0], b_peer(1))
    wait(br1, qr1_recv)
    gp2[left_b, lower] = (gp2[left_b, lower].astype(F32) + br1[...].astype(F32)).astype(BF)
    send(gp2.at[left_b, lower], br2.at[lower], p2_send.at[5], qr2_recv.at[1], b_peer(3))
    for which in range(2):
        wait(bl1, ql2_recv.at[which])
        wait(bl1, qr2_recv.at[which])
    total = gp2[mb].astype(F32) + (bl2[...].astype(F32) + br2[...].astype(F32))
    z3[...] = total.astype(BF).reshape(8, 64, 256)

    for step in range(1, 8):
        send(z3.at[lax.rem(z + step, 8)], zr.at[step - 1], p3_send.at[step - 1], p3_recv.at[step - 1], z_peer(step))
    acc = z3[z].astype(F32)
    for step in range(1, 8):
        wait(zr.at[0], p3_recv.at[step - 1])
        acc = acc + zr[step - 1].astype(F32)
    out[...] = acc

    for k in range(NC):
        wait(three(k, whole(k)), zs_send.at[k])
        wait(six(k, whole(k)), a_send.at[k])
        wait(six(k, half(k, 0)), b_send.at[k])
        wait(core_half(k, 0), c_send.at[k])
    wait(lt.at[0, :, :, 0:T], x_send.at[0])
    wait(lt.at[1, :, :, 0:T], x_send.at[1])
    wait(rg.at[0, :, 3072:4096], x_send.at[2])
    wait(rg.at[0, :, 0:3072], x_send.at[3])
    for which in range(6):
        for i in range(2):
            wait(l1.at[0], p1_send.at[which, i])
        wait(bl1, p2_send.at[which])
    for step in range(7):
        wait(zr.at[0], p3_send.at[step])


def per_device(teacher_tokens, teacher_qkv, teacher_out, student_tokens, student_weights):
    vmem = pltpu.VMEM
    dma = pltpu.SemaphoreType.DMA
    any_spec = pl.BlockSpec(memory_space=pl.ANY)
    return pl.pallas_call(
        kernel,
        out_shape=jax.ShapeDtypeStruct((64, 256), F32),
        in_specs=[any_spec] * 5,
        out_specs=pl.BlockSpec(memory_space=pltpu.VMEM),
        scratch_shapes=[
            vmem((4, 2, RT, TW), BF),
            vmem((4, 2, RS, SW), BF),
            vmem((T, DT), BF),
            vmem((T, DS), BF),
            vmem((T, DT), BF),
            vmem((T, DS), BF),
            vmem((T, 3 * DT), BF),
            vmem((T, DT), BF),
            vmem((T, 3 * DS), BF),
            vmem((16, T, T), BF),
            vmem((T, DS), BF),
            vmem((T, T), F32),
            vmem((2, 8, 2, 64, T), BF),
            vmem((2, 8, 64, 2 * T), BF),
            vmem((2, T, SW), BF),
            vmem((T, DS), BF),
            vmem((16, 512, 256), BF),
            vmem((2, 512, 256), BF),
            vmem((2, 512, 256), BF),
            vmem((4, 512, 256), BF),
            vmem((4, 512, 256), BF),
            vmem((4, 512, 256), BF),
            vmem((256, 256), BF),
            vmem((256, 256), BF),
            vmem((512, 256), BF),
            vmem((512, 256), BF),
            vmem((8, 64, 256), BF),
            vmem((7, 64, 256), BF),
            dma((5,)),
            dma((NC,)), dma((NC,)),
            dma((NC,)), dma((NC,)), dma((NC,)),
            dma((NC,)), dma((NC,)), dma((NC,)),
            dma((NC,)), dma((NC,)),
            dma((4,)), dma((4,)),
            dma((6, 2)), dma((2,)), dma((2,)), dma((4,)), dma((4,)),
            dma((6,)), dma, dma, dma((2,)), dma((2,)),
            dma((7,)), dma((7,)),
        ],
        compiler_params=pltpu.CompilerParams(
            collective_id=0, has_side_effects=True, vmem_limit_bytes=62 * 1024 * 1024
        ),
        cost_estimate=pl.CostEstimate(flops=11_400_000_000, bytes_accessed=30_000_000, transcendentals=2_700_000),
        name="distill",
    )(teacher_tokens, teacher_qkv, teacher_out, student_tokens, student_weights)


def solution(mesh):
    return jax.shard_map(
        per_device,
        mesh=mesh,
        in_specs=(
            P(("rows", "dp"), None),
            P("rows", None),
            P("rows", None),
            P(("rows", "dp"), None),
            P("rows", None),
        ),
        out_specs=P(("group", "rows"), "dp"),
        check_vma=False,
    )
```

```python
import jax
import jax.numpy as jnp
from jax import lax
from jax.experimental import pallas as pl
from jax.experimental.pallas import tpu as pltpu
from jax.sharding import PartitionSpec as P

MESH = pl.DeviceIdType.MESH
BF = jnp.bfloat16
F32 = jnp.float32

T = 256
DT = 1536
DS = 1024
TW = 4 * DT
SW = 4 * DS
RT = DT // 8
RS = DS // 8
QT = RT // 4
QS = RS // 4
EPS = 1e-06
EXP2_SCALE = 0.125 * 1.4426950408889634

CHUNKS = (
    [(True, 0, 256), (True, 256, 512)]
    + [(True, 768 * i, 768) for i in range(1, 6)]
    + [(False, 1024 * i, 1024) for i in range(4)]
    + [(True, 4608, 768), (True, 5376, 512), (True, 5888, 256)]
)
NC = len(CHUNKS)


def mm(a, b, ca=1, cb=0):
    return lax.dot_general(a, b, (((ca,), (cb,)), ((), ())), preferred_element_type=F32)


def kernel(
    tt, tq, to, st, sw, out,
    Wt, Ws, xt, xs, nt, ns, at, mt, as_, ex, iv, ms, rs, uh_ref, ul_ref, gs, gt, tr, lt, rg,
    gp, rx, gp2, bl1, br1, bl2, br2, z3, zr,
    loc_sem, zs_send, zs_recv, a_send, al_recv, ar_recv, b_send, bl_recv, br_recv, c_send, c_recv,
    x_send, x_recv, g_send, g_recv, p1_send, p1_recv,
    p2_send, ql1_recv, qr1_recv, ql2_recv, qr2_recv, p3_send, p3_recv,
):
    g = lax.axis_index("group")
    r = lax.axis_index("rows")
    d = lax.axis_index("dp")
    zl, c = lax.div(r, 2), lax.rem(r, 2)
    z = g * 4 + zl
    x, y = lax.div(d, 4), lax.rem(d, 4)
    oc = 1 - c
    ma = x * oc + y * c
    mb = y * oc + x * c

    def a_peer(step):
        return {"dp": 4 * lax.rem(x + step * oc, 4) + lax.rem(y + step * c, 4)}

    def b_peer(step):
        return {"dp": 4 * lax.rem(x + step * c, 4) + lax.rem(y + step * oc, 4)}

    def z_peer(step):
        far = lax.rem(z + step, 8)
        return {"group": lax.div(far, 4), "rows": 2 * lax.rem(far, 4) + c}

    sibling = {"rows": r + 1 - 2 * c}

    def send(src, dst, send_sem, recv_sem, to_whom):
        pltpu.make_async_remote_copy(
            src_ref=src, dst_ref=dst, send_sem=send_sem, recv_sem=recv_sem,
            device_id=to_whom, device_id_type=MESH,
        ).start()

    def wait(ref, sem):
        pltpu.make_async_copy(ref, ref, sem).wait()

    local = [
        pltpu.make_async_copy(tt.at[pl.ds(g * T, T)], xt, loc_sem.at[0]),
        pltpu.make_async_copy(st.at[pl.ds(g * T, T)], xs, loc_sem.at[1]),
        pltpu.make_async_copy(tq, Wt.at[zl, c, :, 0:4608], loc_sem.at[2]),
        pltpu.make_async_copy(to, Wt.at[zl, c, :, 4608:6144], loc_sem.at[3]),
        pltpu.make_async_copy(sw, Ws.at[zl, c], loc_sem.at[4]),
    ]
    for copy in local:
        copy.start()

    barrier = pltpu.get_barrier_semaphore()
    peers = [z_peer(s) for s in range(1, 8)] + [a_peer(1), a_peer(3), b_peer(1), b_peer(3), sibling]
    for peer in peers:
        pl.semaphore_signal(barrier, inc=1, device_id=peer, device_id_type=MESH)

    def norm(v):
        v = v.astype(F32)
        v = v - jnp.mean(v, axis=-1, keepdims=True)
        s = jnp.mean(v * v, axis=-1, keepdims=True)
        return v * lax.rsqrt(s + EPS)

    local[0].wait()
    nt[...] = norm(xt[...]).astype(BF)
    local[1].wait()
    normed_s = norm(xs[...])
    ns[...] = normed_s.astype(BF)
    tr[0] = normed_s.T.astype(BF).reshape(8, 2, 64, T)
    for copy in local[2:]:
        copy.wait()
    pl.semaphore_wait(barrier, len(peers))

    def piece(chunk, shard, quarter, cols):
        teacher = CHUNKS[chunk][0]
        size = QT if teacher else QS
        rows = pl.ds(pl.multiple_of(quarter * size, 16), size)
        return (Wt if teacher else Ws).at[shard, c, rows, cols]

    def whole(chunk):
        _, first, count = CHUNKS[chunk]
        return slice(first, first + count)

    def half(chunk, which):
        _, first, count = CHUNKS[chunk]
        return slice(first + which * count // 2, first + (which + 1) * count // 2)

    def three(chunk, cols):
        teacher = CHUNKS[chunk][0]
        return (Wt.at[0, 0, 0 : 3 * QT, cols]) if teacher else (Ws.at[0, 0, 0 : 3 * QS, cols])

    def six(chunk, cols):
        teacher = CHUNKS[chunk][0]
        return (Wt.at[0, :, 0 : 3 * QT, cols]) if teacher else (Ws.at[0, :, 0 : 3 * QS, cols])

    def core_half(chunk, core):
        teacher = CHUNKS[chunk][0]
        return (Wt if teacher else Ws).at[:, core, :, whole(chunk)]

    for k in range(NC):
        teacher, first, count = CHUNKS[k]
        size = QT if teacher else QS
        rows = pl.ds(pl.multiple_of(ma * size, 16), size)
        if not teacher:
            src = sw.at[rows, whole(k)]
        elif first < 4608:
            src = tq.at[rows, whole(k)]
        else:
            src = to.at[rows, slice(first - 4608, first - 4608 + count)]
        for step in (1, 7, 2 if k % 2 == 0 else 6):
            send(src, piece(k, zl, ma, whole(k)), zs_send.at[k], zs_recv.at[k], z_peer(step))

    def stage_a(k):
        wait(three(k, whole(k)), zs_recv.at[k])
        for j in (1, 2, 3):
            src = piece(k, lax.rem(zl + j, 4), ma, whole(k))
            send(src, src, a_send.at[k], al_recv.at[k], a_peer(1))
            send(src, src, a_send.at[k], ar_recv.at[k], a_peer(3))

    def stage_b(k):
        wait(three(k, whole(k)), al_recv.at[k])
        for j in (1, 2, 3):
            src = piece(k, lax.rem(zl + j, 4), lax.rem(ma + 3, 4), half(k, 0))
            send(src, src, b_send.at[k], bl_recv.at[k], a_peer(1))
        wait(three(k, whole(k)), ar_recv.at[k])
        for j in (1, 2, 3):
            src = piece(k, lax.rem(zl + j, 4), lax.rem(ma + 1, 4), half(k, 1))
            send(src, src, b_send.at[k], br_recv.at[k], a_peer(3))

    def stage_c(k):
        wait(three(k, half(k, 0)), bl_recv.at[k])
        wait(three(k, half(k, 1)), br_recv.at[k])
        send(core_half(k, c), core_half(k, c), c_send.at[k], c_recv.at[k], sibling)

    def stage_d(k):
        wait(core_half(k, 0), c_recv.at[k])

    progress = [0]

    def pump(upto):
        while progress[0] < upto:
            t = progress[0]
            if t < NC:
                stage_a(t)
            if 0 <= t - 1 < NC:
                stage_b(t - 1)
            if 0 <= t - 2 < NC:
                stage_c(t - 2)
            progress[0] = t + 1

    def ready(k):
        pump(min(k + 4, NC + 2))
        stage_d(k)

    def share_left(which):
        cols = pl.ds(pl.multiple_of(c * T, T), T)
        send(tr.at[which, :, oc], lt.at[which, :, :, cols], x_send.at[which], x_recv.at[which], sibling)
        lt[which, :, :, cols] = tr[which, :, c]

    pump(1)
    share_left(0)

    lane = lax.broadcasted_iota(jnp.int32, (1, 128), 1)
    low_f = jnp.where(lane < 64, 1.0, 0.0).astype(F32)
    high_f = 1.0 - low_f
    low_b, high_b = low_f.astype(BF), high_f.astype(BF)
    zero_b = jnp.zeros((T, 128), BF)

    def lanes(start, count=128):
        return pl.ds(pl.multiple_of(start, 128), count)

    def both(v):
        return jnp.concatenate([v * low_b, v * high_b], axis=0)

    def attend(q, k, v):
        s = mm(both(q), k, 1, 1)
        e = jnp.exp2((s - jnp.max(s, axis=-1, keepdims=True)) * EXP2_SCALE).astype(BF)
        e0, e1 = e[:T], e[T:]
        ones = jnp.concatenate([zero_b + low_b, zero_b + high_b], axis=0)
        right = jnp.concatenate([both(v), ones], axis=1)
        joined = mm(jnp.concatenate([e0, e1], axis=1), right)
        inv = 1.0 / joined[:, 128:]
        return e0, e1, joined[:, :128] * inv, inv

    def teacher_pair(h):
        q, k, v = at[:, lanes(h * 128)], at[:, lanes(DT + h * 128)], at[:, lanes(2 * DT + h * 128)]
        mt[:, lanes(h * 128)] = attend(q, k, v)[2].astype(BF)

    def student_pair(h):
        q, k, v = as_[:, lanes(h * 128)], as_[:, lanes(DS + h * 128)], as_[:, lanes(2 * DS + h * 128)]
        e0, e1, mixed, inv = attend(q, k, v)
        ex[h, 0:T] = e0
        ex[h, T : 2 * T] = e1
        iv[:, lanes(h * 128)] = inv
        ms[:, lanes(h * 128)] = mixed.astype(BF)

    def pairs(fn, first, last):
        def two(i, carry):
            fn(2 * i)
            fn(2 * i + 1)
            return carry

        lax.fori_loop(first // 2, last // 2, two, 0)

    def weights(k, first, count):
        if CHUNKS[k][0]:
            return Wt[:, :, :, first : first + count].reshape(DT, count)
        return Ws[:, :, :, first : first + count].reshape(DS, count)

    for k in range(7):
        ready(k)
        _, first, count = CHUNKS[k]
        for n in range(first, first + count, 256):
            at[:, n : n + 256] = mm(nt[...], weights(k, n, 256)).astype(BF)
    for part in range(3):
        pairs(teacher_pair, 4 * part, 4 * part + 4)
        pump(min(progress[0] + 1, NC + 2))
    for k in range(7, 10):
        ready(k)
        _, first, count = CHUNKS[k]
        for n in range(first, first + count, 256):
            as_[:, n : n + 256] = mm(ns[...], weights(k, n, 256)).astype(BF)
    for part in range(2):
        pairs(student_pair, 4 * part, 4 * part + 4)
        pump(min(progress[0] + 1, NC + 2))
    tr[1] = ms[...].astype(F32).T.astype(BF).reshape(8, 2, 64, T)
    share_left(1)

    ready(10)
    square = jnp.zeros((T, 1), F32)
    for n in range(0, DS, 256):
        res = xs[:, n : n + 256].astype(F32) + mm(ms[...], weights(10, 3072 + n, 256))
        square += jnp.sum(res * res, axis=-1, keepdims=True)
        rs[:, n : n + 256] = res
    scale = lax.rsqrt(square / DS + EPS) * DS**-0.5
    for n in range(0, DS, 256):
        unit = rs[:, n : n + 256] * scale
        rs[:, n : n + 256] = unit
        high = unit.astype(BF)
        uh_ref[:, n : n + 256] = high
        ul_ref[:, n : n + 256] = (unit - high.astype(F32)).astype(BF)
    cross = mm(uh_ref[...], ul_ref[...], 1, 1)
    gs[...] = mm(uh_ref[...], uh_ref[...], 1, 1) + (cross + cross.T)

    square = jnp.zeros((T, 1), F32)
    for k in (11, 12, 13):
        ready(k)
        _, first, count = CHUNKS[k]
        for n in range(first, first + count, 256):
            cols = slice(n - 4608, n - 4608 + 256)
            feats = (xt[:, cols].astype(F32) + mm(mt[...], weights(k, n, 256))).astype(BF)
            wide = feats.astype(F32)
            square += jnp.sum(wide * wide, axis=-1, keepdims=True)
            term = mm(feats, feats, 1, 1)
            if n == 4608:
                gt[...] = term
            else:
                gt[...] += term
    row = lax.rsqrt(square / DT + EPS) * DT**-0.5
    along = jnp.broadcast_to(row, (T, 128)).T[0:1, :]
    diff = 8.0 * (gs[...] - gt[...] * row * along)

    eh = diff.astype(BF)
    el = (diff - eh.astype(F32)).astype(BF)
    du = mm(eh, uh_ref[...]) + mm(jnp.concatenate([eh, el], axis=1), jnp.concatenate([ul_ref[...], uh_ref[...]], axis=0))
    unit = rs[...]
    rg[c, :, 3072:4096] = (scale * (du - jnp.sum(du * unit, axis=-1, keepdims=True) * unit)).astype(BF)
    own_out = rg.at[c, :, 3072:4096]
    send(own_out, own_out, x_send.at[2], x_recv.at[2], sibling)

    def where_to(section, group):
        i = group * oc + section * c
        return lax.rem(section * oc + group * c - ma + 4, 4), i

    def transfer(n, direction, slot):
        send(
            gp.at[n], rx.at[direction, slot], p1_send.at[n], p1_recv.at[direction, slot], a_peer(1 + 2 * direction)
        )

    def emit(section, group):
        n = 4 * section + group
        left = lt[section // 3].reshape(512, 512)
        right = rg[:, :, pl.ds(pl.multiple_of(n * 256, 256), 256)].reshape(512, 256)
        gp[n] = mm(left, right).astype(BF)
        rel, i = where_to(section, group)
        upper = lax.div(i, 2)

        @pl.when(rel == 2)
        def _():
            transfer(n, upper, i - 2 * upper)

        @pl.when((rel == 1) & (i >= 2) | (rel == 3) & (i < 2))
        def _():
            transfer(n, lax.div(rel, 2), 2 + i)

    def settle(section, group):
        n = 4 * section + group
        rel, i = where_to(section, group)
        direction = lax.div(rel, 2)

        @pl.when((rel == 1) & (i < 2) | (rel == 3) & (i >= 2))
        def _():
            slot = i - 2 * direction
            wait(rx.at[0, 0], p1_recv.at[direction, slot])
            gp[n] = (gp[n].astype(F32) + rx[direction, slot].astype(F32)).astype(BF)
            transfer(n, direction, 2 + i)

    def own_cols(core, group):
        return rg.at[core, :, lanes(group * 256, 256)], rg.at[core, :, lanes(DS + group * 256, 256)], rg.at[
            core, :, lanes(2 * DS + group * 256, 256)
        ]

    ones = zero_b + 1.0

    def backward(group):
        first = group * 256
        og = rg[c, :, 3072:4096]
        up = mm(og, Ws[group, :, :, 3072:4096].reshape(256, DS), 1, 1)
        up = up * iv[:, lanes(first, 256)]
        rows = up * ms[:, lanes(first, 256)].astype(F32) * -0.125
        for p in range(2):
            at0 = first + 128 * p
            q, k, v = as_[:, lanes(at0)], as_[:, lanes(DS + at0)], as_[:, lanes(2 * DS + at0)]
            u = up[:, 128 * p : 128 * p + 128]
            grads = both(u.astype(BF))
            left = jnp.concatenate([both((u * 0.125).astype(BF)), both(rows[:, 128 * p : 128 * p + 128].astype(BF))], axis=1)
            dp = mm(left, jnp.concatenate([v, ones], axis=1), 1, 1)
            e = ex[2 * group + p]
            sg = (e.astype(F32) * dp).astype(BF)
            wide = jnp.concatenate([sg[:T], sg[T:]], axis=1)
            rg[c, :, lanes(at0)] = mm(wide, both(k)).astype(BF)
            rg[c, :, lanes(DS + at0)] = mm(sg, both(q), 0, 0).astype(BF)
            rg[c, :, lanes(2 * DS + at0)] = mm(e, grads, 0, 0).astype(BF)
        for section, mine in enumerate(own_cols(c, group)):
            send(mine, mine, g_send.at[group, section], g_recv.at[group, section], sibling)

    def terms(group):
        for section, theirs in enumerate(own_cols(oc, group)):
            wait(theirs, g_recv.at[group, section])
            emit(section, group)

    def nth(k):
        return lax.rem(y + 2 + lax.div(k * (k + 1), 2), 4)

    first_group = lax.rem(y + 2, 4)
    backward(first_group)
    wait(lt.at[0, :, :, 0:T], x_recv.at[0])
    wait(lt.at[1, :, :, 0:T], x_recv.at[1])
    wait(rg.at[0, :, 3072:4096], x_recv.at[2])

    def emit_out(k, carry):
        emit(3, nth(k))
        return carry

    lax.fori_loop(0, 4, emit_out, 0)
    terms(first_group)

    def later(k, carry):
        backward(nth(k))
        terms(nth(k))
        return carry

    lax.fori_loop(1, 4, later, 0)

    def settle_group(k, carry):
        for section in (3, 0, 1, 2):
            settle(section, nth(k))
        return carry

    lax.fori_loop(0, 4, settle_group, 0)

    def close(i):
        n = (4 * ma + i) * oc + (4 * i + ma) * c
        wait(rx.at[0, 0], p1_recv.at[0, 2 + i])
        wait(rx.at[0, 0], p1_recv.at[1, 2 + i])
        gp2[i] = (gp[n].astype(F32) + (rx[0, 2 + i].astype(F32) + rx[1, 2 + i].astype(F32))).astype(BF)

    far_b, right_b, left_b = lax.rem(mb + 2, 4), lax.rem(mb + 1, 4), lax.rem(mb + 3, 4)
    upper, lower = slice(0, 256), slice(256, 512)
    close(far_b)
    send(gp2.at[far_b, upper], bl1, p2_send.at[0], ql1_recv, b_peer(1))
    send(gp2.at[far_b, lower], br1, p2_send.at[1], qr1_recv, b_peer(3))
    close(right_b)
    send(gp2.at[right_b, lower], bl2.at[lower], p2_send.at[2], ql2_recv.at[1], b_peer(1))
    close(left_b)
    send(gp2.at[left_b, upper], br2.at[upper], p2_send.at[3], qr2_recv.at[0], b_peer(3))
    close(mb)
    wait(bl1, ql1_recv)
    gp2[right_b, upper] = (gp2[right_b, upper].astype(F32) + bl1[...].astype(F32)).astype(BF)
    send(gp2.at[right_b, upper], bl2.at[upper], p2_send.at[4], ql2_recv.at[0], b_peer(1))
    wait(br1, qr1_recv)
    gp2[left_b, lower] = (gp2[left_b, lower].astype(F32) + br1[...].astype(F32)).astype(BF)
    send(gp2.at[left_b, lower], br2.at[lower], p2_send.at[5], qr2_recv.at[1], b_peer(3))
    for which in range(2):
        wait(bl1, ql2_recv.at[which])
        wait(bl1, qr2_recv.at[which])
    total = gp2[mb].astype(F32) + (bl2[...].astype(F32) + br2[...].astype(F32))
    z3[...] = total.astype(BF).reshape(8, 64, 256)

    for step in range(1, 8):
        send(z3.at[lax.rem(z + step, 8)], zr.at[step - 1], p3_send.at[step - 1], p3_recv.at[step - 1], z_peer(step))
    acc = z3[z].astype(F32)
    for step in range(1, 8):
        wait(zr.at[0], p3_recv.at[step - 1])
        acc = acc + zr[step - 1].astype(F32)
    out[...] = acc

    for k in range(NC):
        wait(three(k, whole(k)), zs_send.at[k])
        wait(six(k, whole(k)), a_send.at[k])
        wait(six(k, half(k, 0)), b_send.at[k])
        wait(core_half(k, 0), c_send.at[k])
    wait(lt.at[0, :, :, 0:T], x_send.at[0])
    wait(lt.at[1, :, :, 0:T], x_send.at[1])
    wait(rg.at[0, :, 3072:4096], x_send.at[2])
    for group in range(4):
        for section, mine in enumerate(own_cols(0, group)):
            wait(mine, g_send.at[group, section])

    def sent(n, carry):
        rel, _ = where_to(lax.div(n, 4), lax.rem(n, 4))

        @pl.when(rel != 0)
        def _():
            wait(rx.at[0, 0], p1_send.at[n])

        return carry

    lax.fori_loop(0, 16, sent, 0)
    for which in range(6):
        wait(bl1, p2_send.at[which])
    for step in range(7):
        wait(zr.at[0], p3_send.at[step])


def per_device(teacher_tokens, teacher_qkv, teacher_out, student_tokens, student_weights):
    vmem = pltpu.VMEM
    dma = pltpu.SemaphoreType.DMA
    any_spec = pl.BlockSpec(memory_space=pl.ANY)
    return pl.pallas_call(
        kernel,
        out_shape=jax.ShapeDtypeStruct((64, 256), F32),
        in_specs=[any_spec] * 5,
        out_specs=pl.BlockSpec(memory_space=pltpu.VMEM),
        scratch_shapes=[
            vmem((4, 2, RT, TW), BF),
            vmem((4, 2, RS, SW), BF),
            vmem((T, DT), BF),
            vmem((T, DS), BF),
            vmem((T, DT), BF),
            vmem((T, DS), BF),
            vmem((T, 3 * DT), BF),
            vmem((T, DT), BF),
            vmem((T, 3 * DS), BF),
            vmem((8, 2 * T, T), BF),
            vmem((T, DS), F32),
            vmem((T, DS), BF),
            vmem((T, DS), F32),
            vmem((T, DS), BF),
            vmem((T, DS), BF),
            vmem((T, T), F32),
            vmem((T, T), F32),
            vmem((2, 8, 2, 64, T), BF),
            vmem((2, 8, 64, 2 * T), BF),
            vmem((2, T, SW), BF),
            vmem((16, 512, 256), BF),
            vmem((2, 6, 512, 256), BF),
            vmem((4, 512, 256), BF),
            vmem((256, 256), BF),
            vmem((256, 256), BF),
            vmem((512, 256), BF),
            vmem((512, 256), BF),
            vmem((8, 64, 256), BF),
            vmem((7, 64, 256), BF),
            dma((5,)),
            dma((NC,)), dma((NC,)),
            dma((NC,)), dma((NC,)), dma((NC,)),
            dma((NC,)), dma((NC,)), dma((NC,)),
            dma((NC,)), dma((NC,)),
            dma((3,)), dma((3,)),
            dma((4, 3)), dma((4, 3)),
            dma((16,)), dma((2, 6)),
            dma((6,)), dma, dma, dma((2,)), dma((2,)),
            dma((7,)), dma((7,)),
        ],
        compiler_params=pltpu.CompilerParams(
            collective_id=0, has_side_effects=True, vmem_limit_bytes=62 * 1024 * 1024
        ),
        cost_estimate=pl.CostEstimate(flops=11_400_000_000, bytes_accessed=30_000_000, transcendentals=2_700_000),
        name="distill",
    )(teacher_tokens, teacher_qkv, teacher_out, student_tokens, student_weights)


def solution(mesh):
    return jax.shard_map(
        per_device,
        mesh=mesh,
        in_specs=(
            P(("rows", "dp"), None),
            P("rows", None),
            P("rows", None),
            P(("rows", "dp"), None),
            P("rows", None),
        ),
        out_specs=P(("group", "rows"), "dp"),
        check_vma=False,
    )
```

```python
import functools

import jax
import jax.numpy as jnp
from jax import lax
from jax.experimental import pallas as pl
from jax.experimental.pallas import tpu as pltpu
from jax.sharding import PartitionSpec as P

MESH = pl.DeviceIdType.MESH
BF = jnp.bfloat16
F32 = jnp.float32

T = 256
DT = 1536
DS = 1024
TW = 4 * DT
SW = 4 * DS
RT = DT // 8
RS = DS // 8
QT = RT // 4
QS = RS // 4
EPS = 1e-06
EXP2_SCALE = 0.125 * 1.4426950408889634

CHUNKS = (
    [(True, 0, 256, True), (True, 256, 512, True)]
    + [(True, 768 * i, 768, True) for i in range(1, 6)]
    + [(False, 1024 * i, 1024, True) for i in range(4)]
    + [(True, 4608, 768, True), (True, 5376, 512, False), (True, 5888, 256, False)]
)
NC = len(CHUNKS)


WINDOW = 3
SLACK = 0.0
Z_RATE, RING_RATE, CORE_RATE, HOP = 85e3, 80e3, 500e3, 1.5


def plan(tasks):
    z_free, ring_free, core_free = 0.0, 0.0, 0.0
    events, pending = [], [(0.0, 0, k) for k in range(WINDOW)]
    while pending:
        pending.sort()
        when, stage, k = pending.pop(0)
        teacher, _, count, ring = CHUNKS[k]
        size = (RT if teacher else RS) * count * 2
        if stage == 0:
            z_free = max(z_free, when) + 2 * (size // 4 if ring else size) / Z_RATE
            events.append((z_free + HOP, 1, k))
            pending.append((z_free + HOP, 1, k))
            if k + WINDOW < NC:
                pending.append((z_free + HOP, 0, k + WINDOW))
        elif stage == 1:
            z_free = max(z_free, when) + (size // 4 if ring else size) / Z_RATE
            events.append((z_free + HOP, 2, k))
            pending.append((z_free + HOP, 2 if ring else 4, k))
        elif stage == 2:
            ring_free = max(ring_free, when) + 0.75 * size / RING_RATE
            events.append((ring_free + HOP, 3, k))
            pending.append((ring_free + HOP, 3, k))
        elif stage == 3:
            ring_free = max(ring_free, when) + 0.375 * size / RING_RATE
            pending.append((ring_free + HOP, 4, k))
        else:
            events.append((when, 4, k))
            core_free = max(core_free, when) + 4 * size / CORE_RATE
            events.append((core_free + HOP, 5, k))
    events.sort()
    order, clock, ready = [], 0.0, set()
    for index, (need, cost) in enumerate(tasks):
        while events and (events[0][0] <= clock + cost - SLACK or (need is not None and need not in ready)):
            when, stage, k = events.pop(0)
            clock = max(clock, when)
            order.append((stage, k))
            if stage == 5:
                ready.add(k)
        order.append((0, index))
        clock += cost
    return order


def mm(a, b, ca=1, cb=0):
    return lax.dot_general(a, b, (((ca,), (cb,)), ((), ())), preferred_element_type=F32)


def kernel(
    tt, tq, to, st, sw, out,
    Wt, Ws, xt, xs, nt, ns, at, mt, as_, ex, iv, ms, rs, uh_ref, ul_ref, gs, gt, tr, lt, rg,
    gp, rx, gp2, bl1, br1, bl2, br2, z3, zr,
    loc_sem, z_send, zl_recv, zr_recv, z2_send, zf_recv, zg_recv,
    a_send, al_recv, ar_recv, b_send, bl_recv, br_recv, c_send, c_recv,
    x_send, x_recv, g_send, g_recv, p1_send, p1_recv,
    p2_send, ql1_recv, qr1_recv, ql2_recv, qr2_recv, p3_send, p3_recv,
):
    g = lax.axis_index("group")
    r = lax.axis_index("rows")
    d = lax.axis_index("dp")
    zl, c = lax.div(r, 2), lax.rem(r, 2)
    z = g * 4 + zl
    x, y = lax.div(d, 4), lax.rem(d, 4)
    oc = 1 - c
    ma = x * oc + y * c
    mb = y * oc + x * c

    def a_peer(step):
        return {"dp": 4 * lax.rem(x + step * oc, 4) + lax.rem(y + step * c, 4)}

    def b_peer(step):
        return {"dp": 4 * lax.rem(x + step * c, 4) + lax.rem(y + step * oc, 4)}

    def z_peer(step):
        far = lax.rem(z + step, 8)
        return {"group": lax.div(far, 4), "rows": 2 * lax.rem(far, 4) + c}

    sibling = {"rows": r + 1 - 2 * c}

    def send(src, dst, send_sem, recv_sem, to_whom):
        pltpu.make_async_remote_copy(
            src_ref=src, dst_ref=dst, send_sem=send_sem, recv_sem=recv_sem,
            device_id=to_whom, device_id_type=MESH,
        ).start()

    def wait(ref, sem):
        pltpu.make_async_copy(ref, ref, sem).wait()

    local = [
        pltpu.make_async_copy(tt.at[pl.ds(g * T, T)], xt, loc_sem.at[0]),
        pltpu.make_async_copy(st.at[pl.ds(g * T, T)], xs, loc_sem.at[1]),
        pltpu.make_async_copy(tq, Wt.at[zl, c, :, 0:4608], loc_sem.at[2]),
        pltpu.make_async_copy(to, Wt.at[zl, c, :, 4608:6144], loc_sem.at[3]),
        pltpu.make_async_copy(sw, Ws.at[zl, c], loc_sem.at[4]),
    ]
    for copy in local:
        copy.start()

    barrier = pltpu.get_barrier_semaphore()
    peers = [z_peer(s) for s in range(1, 8)] + [a_peer(1), a_peer(3), b_peer(1), b_peer(3), sibling]
    for peer in peers:
        pl.semaphore_signal(barrier, inc=1, device_id=peer, device_id_type=MESH)

    def norm(v):
        v = v.astype(F32)
        v = v - jnp.mean(v, axis=-1, keepdims=True)
        s = jnp.mean(v * v, axis=-1, keepdims=True)
        return v * lax.rsqrt(s + EPS)

    local[0].wait()
    nt[...] = norm(xt[...]).astype(BF)
    local[1].wait()
    normed_s = norm(xs[...])
    ns[...] = normed_s.astype(BF)
    tr[0] = normed_s.T.astype(BF).reshape(8, 2, 64, T)
    for copy in local[2:]:
        copy.wait()
    pl.semaphore_wait(barrier, len(peers))

    def size_of(k):
        teacher, _, _, ring = CHUNKS[k]
        full = RT if teacher else RS
        return full // 4 if ring else full

    def buffer(k):
        return Wt if CHUNKS[k][0] else Ws

    def piece(k, shard, quarter, cols):
        size = size_of(k)
        rows = pl.ds(pl.multiple_of(quarter * size, 16), size) if CHUNKS[k][3] else slice(0, size)
        return buffer(k).at[shard, c, rows, cols]

    def part(k, which=None):
        _, first, count, _ = CHUNKS[k]
        if which is None:
            return slice(first, first + count)
        return slice(first + which * count // 2, first + (which + 1) * count // 2)

    def some(k, pieces, cols):
        rows = pieces * size_of(k)
        full = RT if CHUNKS[k][0] else RS
        if rows <= full:
            return buffer(k).at[0, 0, 0:rows, cols]
        if rows == pieces * full:
            return buffer(k).at[0:pieces, 0, :, cols]
        return buffer(k).at[0, :, 0 : rows // 2, cols]

    def core_half(k, core):
        return buffer(k).at[:, core, :, part(k)]

    up_z, down_z = lax.rem(zl + 1, 4), lax.rem(zl + 3, 4)
    opposite = lax.rem(zl + 2, 4)

    def stage_0(k):
        teacher, first, count, ring = CHUNKS[k]
        size = size_of(k)
        rows = pl.ds(pl.multiple_of(ma * size, 16), size) if ring else slice(0, size)
        if not teacher:
            src = sw.at[rows, part(k)]
        elif first < 4608:
            src = tq.at[rows, part(k)]
        else:
            src = to.at[rows, slice(first - 4608, first - 4608 + count)]
        dst = piece(k, zl, ma, part(k))
        send(src, dst, z_send.at[k], zl_recv.at[k], z_peer(1))
        send(src, dst, z_send.at[k], zr_recv.at[k], z_peer(7))

    def spread(k, shard):
        src = piece(k, shard, ma, part(k))
        send(src, src, a_send.at[k], al_recv.at[k], a_peer(1))
        send(src, src, a_send.at[k], ar_recv.at[k], a_peer(3))

    def stage_1(k):
        if k + WINDOW < NC:
            stage_0(k + WINDOW)
        for recv, relay, shard, which, step in ((zl_recv, zf_recv, down_z, 0, 1), (zr_recv, zg_recv, up_z, 1, 7)):
            wait(some(k, 1, part(k)), recv.at[k])
            src = piece(k, shard, ma, part(k, which))
            send(src, src, z2_send.at[k], relay.at[k], z_peer(step))
            if CHUNKS[k][3]:
                spread(k, shard)

    def stage_2(k):
        wait(some(k, 1, part(k, 0)), zf_recv.at[k])
        wait(some(k, 1, part(k, 1)), zg_recv.at[k])
        if CHUNKS[k][3]:
            spread(k, opposite)

    def stage_3(k):
        if not CHUNKS[k][3]:
            return
        for recv, relay, step, which in ((al_recv, bl_recv, 1, 0), (ar_recv, br_recv, 3, 1)):
            wait(some(k, 3, part(k)), recv.at[k])
            for shard in (up_z, opposite, down_z):
                src = piece(k, shard, lax.rem(ma + 4 - step, 4), part(k, which))
                send(src, src, b_send.at[k], relay.at[k], a_peer(step))

    def stage_4(k):
        if CHUNKS[k][3]:
            wait(some(k, 3, part(k, 0)), bl_recv.at[k])
            wait(some(k, 3, part(k, 1)), br_recv.at[k])
        send(core_half(k, c), core_half(k, c), c_send.at[k], c_recv.at[k], sibling)

    def stage_5(k):
        wait(core_half(k, 0), c_recv.at[k])

    for k in range(WINDOW):
        stage_0(k)

    def share_left(which):
        cols = pl.ds(pl.multiple_of(c * T, T), T)
        send(tr.at[which, :, oc], lt.at[which, :, :, cols], x_send.at[which], x_recv.at[which], sibling)
        lt[which, :, :, cols] = tr[which, :, c]

    share_left(0)

    lane = lax.broadcasted_iota(jnp.int32, (1, 128), 1)
    low_f = jnp.where(lane < 64, 1.0, 0.0).astype(F32)
    high_f = 1.0 - low_f
    low_b, high_b = low_f.astype(BF), high_f.astype(BF)
    zero_b = jnp.zeros((T, 128), BF)

    def lanes(start, count=128):
        return pl.ds(pl.multiple_of(start, 128), count)

    def both(v):
        return jnp.concatenate([v * low_b, v * high_b], axis=0)

    def attend(q, k, v):
        s = mm(both(q), k, 1, 1)
        e = jnp.exp2((s - jnp.max(s, axis=-1, keepdims=True)) * EXP2_SCALE).astype(BF)
        e0, e1 = e[:T], e[T:]
        ones = jnp.concatenate([zero_b + low_b, zero_b + high_b], axis=0)
        right = jnp.concatenate([both(v), ones], axis=1)
        joined = mm(jnp.concatenate([e0, e1], axis=1), right)
        inv = 1.0 / joined[:, 128:]
        return e0, e1, joined[:, :128] * inv, inv

    def teacher_pair(h):
        q, k, v = at[:, lanes(h * 128)], at[:, lanes(DT + h * 128)], at[:, lanes(2 * DT + h * 128)]
        mt[:, lanes(h * 128)] = attend(q, k, v)[2].astype(BF)

    def student_pair(h):
        q, k, v = as_[:, lanes(h * 128)], as_[:, lanes(DS + h * 128)], as_[:, lanes(2 * DS + h * 128)]
        e0, e1, mixed, inv = attend(q, k, v)
        ex[h, 0:T] = e0
        ex[h, T : 2 * T] = e1
        iv[:, lanes(h * 128)] = inv
        ms[:, lanes(h * 128)] = mixed.astype(BF)

    def weights(k, first, count):
        if CHUNKS[k][0]:
            return Wt[:, :, :, first : first + count].reshape(DT, count)
        return Ws[:, :, :, first : first + count].reshape(DS, count)

    state = {}

    def tiles(k):
        _, first, count, _ = CHUNKS[k]
        return range(first, first + count, 256)

    def project_teacher(k, n):
        at[:, n : n + 256] = mm(nt[...], weights(k, n, 256)).astype(BF)

    def project_student(k, n):
        as_[:, n : n + 256] = mm(ns[...], weights(k, n, 256)).astype(BF)

    def share_mixed():
        tr[1] = ms[...].astype(F32).T.astype(BF).reshape(8, 2, 64, T)
        share_left(1)

    def result(k, n):
        n = n - 3 * DS
        res = xs[:, n : n + 256].astype(F32) + mm(ms[...], weights(k, 3 * DS + n, 256))
        square = jnp.sum(res * res, axis=-1, keepdims=True)
        rs[:, n : n + 256] = res
        state["result"] = square if n == 0 else state["result"] + square

    def student_unit():
        state["scale"] = lax.rsqrt(state["result"] / DS + EPS) * DS**-0.5
        for n in range(0, DS, 256):
            unit = rs[:, n : n + 256] * state["scale"]
            rs[:, n : n + 256] = unit
            high = unit.astype(BF)
            uh_ref[:, n : n + 256] = high
            ul_ref[:, n : n + 256] = (unit - high.astype(F32)).astype(BF)

    def student_cross():
        cross = mm(uh_ref[...], ul_ref[...], 1, 1)
        gs[...] = cross + cross.T

    def student_gram():
        gs[...] += mm(uh_ref[...], uh_ref[...], 1, 1)

    def features(k, n):
        cols = slice(n - 4608, n - 4608 + 256)
        feats = (xt[:, cols].astype(F32) + mm(mt[...], weights(k, n, 256))).astype(BF)
        wide = feats.astype(F32)
        square = jnp.sum(wide * wide, axis=-1, keepdims=True)
        term = mm(feats, feats, 1, 1)
        gt[...] = term if n == 4608 else gt[...] + term
        state["square"] = square if n == 4608 else state["square"] + square

    bind = functools.partial
    tasks = (
        [(k, 0.1, bind(project_teacher, k, n)) for k in range(7) for n in tiles(k)]
        + [(None, 0.35, bind(teacher_pair, h)) for h in range(12)]
        + [(k, 0.15, bind(project_student, k, n)) for k in range(7, 10) for n in tiles(k)]
        + [(None, 0.4, bind(student_pair, h)) for h in range(8)]
        + [(None, 0.5, share_mixed)]
        + [(10, 0.25, bind(result, 10, n)) for n in tiles(10)]
        + [(None, 0.5, student_unit), (None, 0.4, student_cross), (None, 0.2, student_gram)]
        + [(k, 0.4, bind(features, k, n)) for k in range(11, NC) for n in tiles(k)]
    )
    steps = {1: stage_1, 2: stage_2, 3: stage_3, 4: stage_4, 5: stage_5}
    for stage, index in plan([task[:2] for task in tasks]):
        if stage:
            steps[stage](index)
        else:
            tasks[index][2]()
    scale, square = state["scale"], state["square"]
    row = lax.rsqrt(square / DT + EPS) * DT**-0.5
    along = jnp.broadcast_to(row, (T, 128)).T[0:1, :]
    diff = 8.0 * (gs[...] - gt[...] * row * along)

    eh = diff.astype(BF)
    el = (diff - eh.astype(F32)).astype(BF)
    du = mm(eh, uh_ref[...]) + mm(jnp.concatenate([eh, el], axis=1), jnp.concatenate([ul_ref[...], uh_ref[...]], axis=0))
    unit = rs[...]
    rg[c, :, 3072:4096] = (scale * (du - jnp.sum(du * unit, axis=-1, keepdims=True) * unit)).astype(BF)
    own_out = rg.at[c, :, 3072:4096]
    send(own_out, own_out, x_send.at[2], x_recv.at[2], sibling)

    def where_to(section, group):
        i = group * oc + section * c
        return lax.rem(section * oc + group * c - ma + 4, 4), i

    def transfer(n, direction, slot):
        send(
            gp.at[n], rx.at[direction, slot], p1_send.at[n], p1_recv.at[direction, slot], a_peer(1 + 2 * direction)
        )

    def emit(section, group):
        n = 4 * section + group
        left = lt[section // 3].reshape(512, 512)
        right = rg[:, :, pl.ds(pl.multiple_of(n * 256, 256), 256)].reshape(512, 256)
        gp[n] = mm(left, right).astype(BF)
        rel, i = where_to(section, group)
        upper = lax.div(i, 2)

        @pl.when(rel == 2)
        def _():
            transfer(n, upper, i - 2 * upper)

        @pl.when((rel == 1) & (i >= 2) | (rel == 3) & (i < 2))
        def _():
            transfer(n, lax.div(rel, 2), 2 + i)

    def settle(section, group):
        n = 4 * section + group
        rel, i = where_to(section, group)
        direction = lax.div(rel, 2)

        @pl.when((rel == 1) & (i < 2) | (rel == 3) & (i >= 2))
        def _():
            slot = i - 2 * direction
            wait(rx.at[0, 0], p1_recv.at[direction, slot])
            gp[n] = (gp[n].astype(F32) + rx[direction, slot].astype(F32)).astype(BF)
            transfer(n, direction, 2 + i)

    def own_cols(core, group):
        return rg.at[core, :, lanes(group * 256, 256)], rg.at[core, :, lanes(DS + group * 256, 256)], rg.at[
            core, :, lanes(2 * DS + group * 256, 256)
        ]

    ones = zero_b + 1.0

    def backward(group):
        first = group * 256
        og = rg[c, :, 3072:4096]
        up = mm(og, Ws[group, :, :, 3072:4096].reshape(256, DS), 1, 1)
        up = up * iv[:, lanes(first, 256)]
        rows = up * ms[:, lanes(first, 256)].astype(F32) * -0.125
        for p in range(2):
            at0 = first + 128 * p
            q, k, v = as_[:, lanes(at0)], as_[:, lanes(DS + at0)], as_[:, lanes(2 * DS + at0)]
            u = up[:, 128 * p : 128 * p + 128]
            grads = both(u.astype(BF))
            left = jnp.concatenate([both((u * 0.125).astype(BF)), both(rows[:, 128 * p : 128 * p + 128].astype(BF))], axis=1)
            dp = mm(left, jnp.concatenate([v, ones], axis=1), 1, 1)
            e = ex[2 * group + p]
            sg = (e.astype(F32) * dp).astype(BF)
            wide = jnp.concatenate([sg[:T], sg[T:]], axis=1)
            rg[c, :, lanes(at0)] = mm(wide, both(k)).astype(BF)
            rg[c, :, lanes(DS + at0)] = mm(sg, both(q), 0, 0).astype(BF)
            rg[c, :, lanes(2 * DS + at0)] = mm(e, grads, 0, 0).astype(BF)
        for section, mine in enumerate(own_cols(c, group)):
            send(mine, mine, g_send.at[group, section], g_recv.at[group, section], sibling)

    def terms(group):
        for section, theirs in enumerate(own_cols(oc, group)):
            wait(theirs, g_recv.at[group, section])
            emit(section, group)

    def nth(k):
        return lax.rem(y + 2 + lax.div(k * (k + 1), 2), 4)

    first_group = lax.rem(y + 2, 4)
    backward(first_group)
    wait(lt.at[0, :, :, 0:T], x_recv.at[0])
    wait(lt.at[1, :, :, 0:T], x_recv.at[1])
    wait(rg.at[0, :, 3072:4096], x_recv.at[2])

    def emit_out(k, carry):
        emit(3, nth(k))
        return carry

    lax.fori_loop(0, 4, emit_out, 0)
    terms(first_group)

    def later(k, carry):
        backward(nth(k))
        terms(nth(k))
        return carry

    lax.fori_loop(1, 4, later, 0)

    def settle_group(k, carry):
        for section in (3, 0, 1, 2):
            settle(section, nth(k))
        return carry

    lax.fori_loop(0, 4, settle_group, 0)

    def close(i):
        n = (4 * ma + i) * oc + (4 * i + ma) * c
        wait(rx.at[0, 0], p1_recv.at[0, 2 + i])
        wait(rx.at[0, 0], p1_recv.at[1, 2 + i])
        gp2[i] = (gp[n].astype(F32) + (rx[0, 2 + i].astype(F32) + rx[1, 2 + i].astype(F32))).astype(BF)

    far_b, right_b, left_b = lax.rem(mb + 2, 4), lax.rem(mb + 1, 4), lax.rem(mb + 3, 4)
    upper, lower = slice(0, 256), slice(256, 512)
    close(far_b)
    send(gp2.at[far_b, upper], bl1, p2_send.at[0], ql1_recv, b_peer(1))
    send(gp2.at[far_b, lower], br1, p2_send.at[1], qr1_recv, b_peer(3))
    close(right_b)
    send(gp2.at[right_b, lower], bl2.at[lower], p2_send.at[2], ql2_recv.at[1], b_peer(1))
    close(left_b)
    send(gp2.at[left_b, upper], br2.at[upper], p2_send.at[3], qr2_recv.at[0], b_peer(3))
    close(mb)
    wait(bl1, ql1_recv)
    gp2[right_b, upper] = (gp2[right_b, upper].astype(F32) + bl1[...].astype(F32)).astype(BF)
    send(gp2.at[right_b, upper], bl2.at[upper], p2_send.at[4], ql2_recv.at[0], b_peer(1))
    wait(br1, qr1_recv)
    gp2[left_b, lower] = (gp2[left_b, lower].astype(F32) + br1[...].astype(F32)).astype(BF)
    send(gp2.at[left_b, lower], br2.at[lower], p2_send.at[5], qr2_recv.at[1], b_peer(3))
    for which in range(2):
        wait(bl1, ql2_recv.at[which])
        wait(bl1, qr2_recv.at[which])
    total = gp2[mb].astype(F32) + (bl2[...].astype(F32) + br2[...].astype(F32))
    z3[...] = total.astype(BF).reshape(8, 64, 256)

    for step in range(1, 8):
        send(z3.at[lax.rem(z + step, 8)], zr.at[step - 1], p3_send.at[step - 1], p3_recv.at[step - 1], z_peer(step))
    acc = z3[z].astype(F32)
    for step in range(1, 8):
        wait(zr.at[0], p3_recv.at[step - 1])
        acc = acc + zr[step - 1].astype(F32)
    out[...] = acc

    for k in range(NC):
        wait(some(k, 2, part(k)), z_send.at[k])
        wait(some(k, 1, part(k)), z2_send.at[k])
        if CHUNKS[k][3]:
            wait(some(k, 6, part(k)), a_send.at[k])
            wait(some(k, 6, part(k, 0)), b_send.at[k])
        wait(core_half(k, 0), c_send.at[k])
    wait(lt.at[0, :, :, 0:T], x_send.at[0])
    wait(lt.at[1, :, :, 0:T], x_send.at[1])
    wait(rg.at[0, :, 3072:4096], x_send.at[2])
    for group in range(4):
        for section, mine in enumerate(own_cols(0, group)):
            wait(mine, g_send.at[group, section])

    def sent(n, carry):
        rel, _ = where_to(lax.div(n, 4), lax.rem(n, 4))

        @pl.when(rel != 0)
        def _():
            wait(rx.at[0, 0], p1_send.at[n])

        return carry

    lax.fori_loop(0, 16, sent, 0)
    for which in range(6):
        wait(bl1, p2_send.at[which])
    for step in range(7):
        wait(zr.at[0], p3_send.at[step])


def per_device(teacher_tokens, teacher_qkv, teacher_out, student_tokens, student_weights):
    vmem = pltpu.VMEM
    dma = pltpu.SemaphoreType.DMA
    any_spec = pl.BlockSpec(memory_space=pl.ANY)
    return pl.pallas_call(
        kernel,
        out_shape=jax.ShapeDtypeStruct((64, 256), F32),
        in_specs=[any_spec] * 5,
        out_specs=pl.BlockSpec(memory_space=pltpu.VMEM),
        scratch_shapes=[
            vmem((4, 2, RT, TW), BF),
            vmem((4, 2, RS, SW), BF),
            vmem((T, DT), BF),
            vmem((T, DS), BF),
            vmem((T, DT), BF),
            vmem((T, DS), BF),
            vmem((T, 3 * DT), BF),
            vmem((T, DT), BF),
            vmem((T, 3 * DS), BF),
            vmem((8, 2 * T, T), BF),
            vmem((T, DS), F32),
            vmem((T, DS), BF),
            vmem((T, DS), F32),
            vmem((T, DS), BF),
            vmem((T, DS), BF),
            vmem((T, T), F32),
            vmem((T, T), F32),
            vmem((2, 8, 2, 64, T), BF),
            vmem((2, 8, 64, 2 * T), BF),
            vmem((2, T, SW), BF),
            vmem((16, 512, 256), BF),
            vmem((2, 6, 512, 256), BF),
            vmem((4, 512, 256), BF),
            vmem((256, 256), BF),
            vmem((256, 256), BF),
            vmem((512, 256), BF),
            vmem((512, 256), BF),
            vmem((8, 64, 256), BF),
            vmem((7, 64, 256), BF),
            dma((5,)),
            dma((NC,)), dma((NC,)), dma((NC,)), dma((NC,)), dma((NC,)), dma((NC,)),
            dma((NC,)), dma((NC,)), dma((NC,)),
            dma((NC,)), dma((NC,)), dma((NC,)),
            dma((NC,)), dma((NC,)),
            dma((3,)), dma((3,)),
            dma((4, 3)), dma((4, 3)),
            dma((16,)), dma((2, 6)),
            dma((6,)), dma, dma, dma((2,)), dma((2,)),
            dma((7,)), dma((7,)),
        ],
        compiler_params=pltpu.CompilerParams(
            collective_id=0, has_side_effects=True, vmem_limit_bytes=62 * 1024 * 1024
        ),
        cost_estimate=pl.CostEstimate(flops=11_400_000_000, bytes_accessed=30_000_000, transcendentals=2_700_000),
        name="distill",
    )(teacher_tokens, teacher_qkv, teacher_out, student_tokens, student_weights)


def solution(mesh):
    return jax.shard_map(
        per_device,
        mesh=mesh,
        in_specs=(
            P(("rows", "dp"), None),
            P("rows", None),
            P("rows", None),
            P(("rows", "dp"), None),
            P("rows", None),
        ),
        out_specs=P(("group", "rows"), "dp"),
        check_vma=False,
    )
```

```python
import functools

import jax
import jax.numpy as jnp
from jax import lax
from jax.experimental import pallas as pl
from jax.experimental.pallas import tpu as pltpu
from jax.sharding import PartitionSpec as P

MESH = pl.DeviceIdType.MESH
BF = jnp.bfloat16
F32 = jnp.float32

T = 256
DT = 1536
DS = 1024
TW = 4 * DT
SW = 4 * DS
RT = DT // 8
RS = DS // 8
QT = RT // 4
QS = RS // 4
EPS = 1e-06
EXP2_SCALE = 0.125 * 1.4426950408889634

CHUNKS = (
    [(True, 0, 256, True), (True, 256, 512, True)]
    + [(True, 768 * i, 768, True) for i in range(1, 6)]
    + [(False, 1024 * i, 1024, True) for i in range(4)]
    + [(True, 4608, 768, True), (True, 5376, 512, False), (True, 5888, 256, False)]
)
NC = len(CHUNKS)


WINDOW = 3
SLACK = 0.0
Z_RATE, RING_RATE, CORE_RATE, HOP = 85e3, 80e3, 500e3, 1.5


def plan(tasks):
    z_free, ring_free, core_free = 0.0, 0.0, 0.0
    events, pending = [], [(0.0, 0, k) for k in range(WINDOW)]
    while pending:
        pending.sort()
        when, stage, k = pending.pop(0)
        teacher, _, count, ring = CHUNKS[k]
        size = (RT if teacher else RS) * count * 2
        if stage == 0:
            z_free = max(z_free, when) + 2 * (size // 4 if ring else size) / Z_RATE
            events.append((z_free + HOP, 1, k))
            pending.append((z_free + HOP, 1, k))
            if k + WINDOW < NC:
                pending.append((z_free + HOP, 0, k + WINDOW))
        elif stage == 1:
            z_free = max(z_free, when) + (size // 4 if ring else size) / Z_RATE
            events.append((z_free + HOP, 2, k))
            pending.append((z_free + HOP, 2 if ring else 4, k))
        elif stage == 2:
            ring_free = max(ring_free, when) + 0.75 * size / RING_RATE
            events.append((ring_free + HOP, 3, k))
            pending.append((ring_free + HOP, 3, k))
        elif stage == 3:
            ring_free = max(ring_free, when) + 0.375 * size / RING_RATE
            pending.append((ring_free + HOP, 4, k))
        else:
            events.append((when, 4, k))
            core_free = max(core_free, when) + 4 * size / CORE_RATE
            events.append((core_free + HOP, 5, k))
    events.sort()
    order, clock, ready = [], 0.0, set()
    for index, (need, cost) in enumerate(tasks):
        while events and (events[0][0] <= clock + cost - SLACK or (need is not None and need not in ready)):
            when, stage, k = events.pop(0)
            clock = max(clock, when)
            order.append((stage, k))
            if stage == 5:
                ready.add(k)
        order.append((0, index))
        clock += cost
    return order


def mm(a, b, ca=1, cb=0):
    return lax.dot_general(a, b, (((ca,), (cb,)), ((), ())), preferred_element_type=F32)


def kernel(
    tt, tq, to, st, sw, out,
    Wt, Ws, xt, xs, nt, ns, at, mt, as_, ex, iv, ms, rs, uh_ref, ul_ref, gs, gt, tr, lt, rg,
    gp, rx, gp2, bl1, br1, bl2, br2, z3, zr,
    loc_sem, z_send, zl_recv, zr_recv, z2_send, zf_recv, zg_recv,
    a_send, al_recv, ar_recv, b_send, bl_recv, br_recv, c_send, c_recv,
    x_send, x_recv, g_send, g_recv, p1_send, p1_recv,
    p2_send, ql1_recv, qr1_recv, ql2_recv, qr2_recv, p3_send, p3_recv,
):
    g = lax.axis_index("group")
    r = lax.axis_index("rows")
    d = lax.axis_index("dp")
    zl, c = lax.div(r, 2), lax.rem(r, 2)
    z = g * 4 + zl
    x, y = lax.div(d, 4), lax.rem(d, 4)
    oc = 1 - c
    ma = x * oc + y * c
    mb = y * oc + x * c

    def a_peer(step):
        return {"dp": 4 * lax.rem(x + step * oc, 4) + lax.rem(y + step * c, 4)}

    def b_peer(step):
        return {"dp": 4 * lax.rem(x + step * c, 4) + lax.rem(y + step * oc, 4)}

    def z_peer(step):
        far = lax.rem(z + step, 8)
        return {"group": lax.div(far, 4), "rows": 2 * lax.rem(far, 4) + c}

    sibling = {"rows": r + 1 - 2 * c}

    def send(src, dst, send_sem, recv_sem, to_whom):
        pltpu.make_async_remote_copy(
            src_ref=src, dst_ref=dst, send_sem=send_sem, recv_sem=recv_sem,
            device_id=to_whom, device_id_type=MESH,
        ).start()

    def wait(ref, sem):
        pltpu.make_async_copy(ref, ref, sem).wait()

    local = [
        pltpu.make_async_copy(tt.at[pl.ds(g * T, T)], xt, loc_sem.at[0]),
        pltpu.make_async_copy(st.at[pl.ds(g * T, T)], xs, loc_sem.at[1]),
        pltpu.make_async_copy(tq, Wt.at[zl, c, :, 0:4608], loc_sem.at[2]),
        pltpu.make_async_copy(to, Wt.at[zl, c, :, 4608:6144], loc_sem.at[3]),
        pltpu.make_async_copy(sw, Ws.at[zl, c], loc_sem.at[4]),
    ]
    for copy in local:
        copy.start()

    barrier = pltpu.get_barrier_semaphore()
    peers = [z_peer(s) for s in range(1, 8)] + [a_peer(1), a_peer(3), b_peer(1), b_peer(3), sibling]
    for peer in peers:
        pl.semaphore_signal(barrier, inc=1, device_id=peer, device_id_type=MESH)

    def norm(v):
        v = v.astype(F32)
        v = v - jnp.mean(v, axis=-1, keepdims=True)
        s = jnp.mean(v * v, axis=-1, keepdims=True)
        return v * lax.rsqrt(s + EPS)

    local[0].wait()
    nt[...] = norm(xt[...]).astype(BF)
    local[1].wait()
    normed_s = norm(xs[...])
    ns[...] = normed_s.astype(BF)
    tr[0] = normed_s.T.astype(BF).reshape(8, 2, 64, T)
    for copy in local[2:]:
        copy.wait()
    pl.semaphore_wait(barrier, len(peers))

    def size_of(k):
        teacher, _, _, ring = CHUNKS[k]
        full = RT if teacher else RS
        return full // 4 if ring else full

    def buffer(k):
        return Wt if CHUNKS[k][0] else Ws

    def piece(k, shard, quarter, cols):
        size = size_of(k)
        rows = pl.ds(pl.multiple_of(quarter * size, 16), size) if CHUNKS[k][3] else slice(0, size)
        return buffer(k).at[shard, c, rows, cols]

    def part(k, which=None):
        _, first, count, _ = CHUNKS[k]
        if which is None:
            return slice(first, first + count)
        return slice(first + which * count // 2, first + (which + 1) * count // 2)

    def some(k, pieces, cols):
        rows = pieces * size_of(k)
        full = RT if CHUNKS[k][0] else RS
        if rows <= full:
            return buffer(k).at[0, 0, 0:rows, cols]
        if rows == pieces * full:
            return buffer(k).at[0:pieces, 0, :, cols]
        return buffer(k).at[0, :, 0 : rows // 2, cols]

    def core_half(k, core):
        return buffer(k).at[:, core, :, part(k)]

    up_z, down_z = lax.rem(zl + 1, 4), lax.rem(zl + 3, 4)
    opposite = lax.rem(zl + 2, 4)

    def stage_0(k):
        teacher, first, count, ring = CHUNKS[k]
        size = size_of(k)
        rows = pl.ds(pl.multiple_of(ma * size, 16), size) if ring else slice(0, size)
        if not teacher:
            src = sw.at[rows, part(k)]
        elif first < 4608:
            src = tq.at[rows, part(k)]
        else:
            src = to.at[rows, slice(first - 4608, first - 4608 + count)]
        dst = piece(k, zl, ma, part(k))
        mine = buffer(k).at[zl, c, :, part(k)]
        send(mine, mine, c_send.at[k], c_recv.at[k], sibling)
        send(src, dst, z_send.at[k], zl_recv.at[k], z_peer(1))
        send(src, dst, z_send.at[k], zr_recv.at[k], z_peer(7))

    def spread(k, shard):
        src = piece(k, shard, ma, part(k))
        send(src, src, a_send.at[k], al_recv.at[k], a_peer(1))
        send(src, src, a_send.at[k], ar_recv.at[k], a_peer(3))

    def stage_1(k):
        if k + WINDOW < NC:
            stage_0(k + WINDOW)
        for recv, relay, shard, which, step in ((zl_recv, zf_recv, down_z, 0, 1), (zr_recv, zg_recv, up_z, 1, 7)):
            wait(some(k, 1, part(k)), recv.at[k])
            src = piece(k, shard, ma, part(k, which))
            send(src, src, z2_send.at[k], relay.at[k], z_peer(step))
            if CHUNKS[k][3]:
                spread(k, shard)

    def stage_2(k):
        wait(some(k, 1, part(k, 0)), zf_recv.at[k])
        wait(some(k, 1, part(k, 1)), zg_recv.at[k])
        if CHUNKS[k][3]:
            spread(k, opposite)

    def stage_3(k):
        if not CHUNKS[k][3]:
            return
        for recv, relay, step, which in ((al_recv, bl_recv, 1, 0), (ar_recv, br_recv, 3, 1)):
            wait(some(k, 3, part(k)), recv.at[k])
            for shard in (up_z, opposite, down_z):
                src = piece(k, shard, lax.rem(ma + 4 - step, 4), part(k, which))
                send(src, src, b_send.at[k], relay.at[k], a_peer(step))

    def stage_4(k):
        if CHUNKS[k][3]:
            wait(some(k, 3, part(k, 0)), bl_recv.at[k])
            wait(some(k, 3, part(k, 1)), br_recv.at[k])
        for shard in (down_z, opposite, up_z):
            src = buffer(k).at[shard, c, :, part(k)]
            send(src, src, c_send.at[k], c_recv.at[k], sibling)

    def stage_5(k):
        wait(core_half(k, 0), c_recv.at[k])

    for k in range(WINDOW):
        stage_0(k)

    def share_left(which):
        cols = pl.ds(pl.multiple_of(c * T, T), T)
        send(tr.at[which, :, oc], lt.at[which, :, :, cols], x_send.at[which], x_recv.at[which], sibling)
        lt[which, :, :, cols] = tr[which, :, c]

    share_left(0)

    lane = lax.broadcasted_iota(jnp.int32, (1, 128), 1)
    low_f = jnp.where(lane < 64, 1.0, 0.0).astype(F32)
    high_f = 1.0 - low_f
    low_b, high_b = low_f.astype(BF), high_f.astype(BF)
    zero_b = jnp.zeros((T, 128), BF)

    def lanes(start, count=128):
        return pl.ds(pl.multiple_of(start, 128), count)

    def both(v):
        return jnp.concatenate([v * low_b, v * high_b], axis=0)

    def attend(q, k, v):
        s = mm(both(q), k, 1, 1)
        e = jnp.exp2((s - jnp.max(s, axis=-1, keepdims=True)) * EXP2_SCALE).astype(BF)
        e0, e1 = e[:T], e[T:]
        ones = jnp.concatenate([zero_b + low_b, zero_b + high_b], axis=0)
        right = jnp.concatenate([both(v), ones], axis=1)
        joined = mm(jnp.concatenate([e0, e1], axis=1), right)
        inv = 1.0 / joined[:, 128:]
        return e0, e1, joined[:, :128] * inv, inv

    def teacher_pair(h):
        q, k, v = at[:, lanes(h * 128)], at[:, lanes(DT + h * 128)], at[:, lanes(2 * DT + h * 128)]
        mt[:, lanes(h * 128)] = attend(q, k, v)[2].astype(BF)

    def student_pair(h):
        q, k, v = as_[:, lanes(h * 128)], as_[:, lanes(DS + h * 128)], as_[:, lanes(2 * DS + h * 128)]
        e0, e1, mixed, inv = attend(q, k, v)
        ex[h, 0:T] = e0
        ex[h, T : 2 * T] = e1
        iv[:, lanes(h * 128)] = inv
        ms[:, lanes(h * 128)] = mixed.astype(BF)

    def weights(k, first, count):
        if CHUNKS[k][0]:
            return Wt[:, :, :, first : first + count].reshape(DT, count)
        return Ws[:, :, :, first : first + count].reshape(DS, count)

    state = {}

    def tiles(k):
        _, first, count, _ = CHUNKS[k]
        return range(first, first + count, 256)

    def project_teacher(k, n):
        at[:, n : n + 256] = mm(nt[...], weights(k, n, 256)).astype(BF)

    def project_student(k, n):
        as_[:, n : n + 256] = mm(ns[...], weights(k, n, 256)).astype(BF)

    def share_mixed():
        tr[1] = ms[...].astype(F32).T.astype(BF).reshape(8, 2, 64, T)
        share_left(1)

    def result(k, n):
        n = n - 3 * DS
        res = xs[:, n : n + 256].astype(F32) + mm(ms[...], weights(k, 3 * DS + n, 256))
        square = jnp.sum(res * res, axis=-1, keepdims=True)
        rs[:, n : n + 256] = res
        state["result"] = square if n == 0 else state["result"] + square

    def student_unit():
        state["scale"] = lax.rsqrt(state["result"] / DS + EPS) * DS**-0.5
        for n in range(0, DS, 256):
            unit = rs[:, n : n + 256] * state["scale"]
            rs[:, n : n + 256] = unit
            high = unit.astype(BF)
            uh_ref[:, n : n + 256] = high
            ul_ref[:, n : n + 256] = (unit - high.astype(F32)).astype(BF)

    def student_cross():
        cross = mm(uh_ref[...], ul_ref[...], 1, 1)
        gs[...] = cross + cross.T

    def student_gram():
        gs[...] += mm(uh_ref[...], uh_ref[...], 1, 1)

    def features(k, n):
        cols = slice(n - 4608, n - 4608 + 256)
        feats = (xt[:, cols].astype(F32) + mm(mt[...], weights(k, n, 256))).astype(BF)
        wide = feats.astype(F32)
        square = jnp.sum(wide * wide, axis=-1, keepdims=True)
        term = mm(feats, feats, 1, 1)
        gt[...] = term if n == 4608 else gt[...] + term
        state["square"] = square if n == 4608 else state["square"] + square

    bind = functools.partial

    def chunks(teacher, first, last):
        return [k for k in range(NC) if CHUNKS[k][0] == teacher and first <= CHUNKS[k][1] < last]

    tasks = (
        [(k, 0.1, bind(project_teacher, k, n)) for k in chunks(True, 0, 3 * DT) for n in tiles(k)]
        + [(None, 0.35, bind(teacher_pair, h)) for h in range(12)]
        + [(k, 0.15, bind(project_student, k, n)) for k in chunks(False, 0, 3 * DS) for n in tiles(k)]
        + [(None, 0.4, bind(student_pair, h)) for h in range(8)]
        + [(None, 0.5, share_mixed)]
        + [(k, 0.25, bind(result, k, n)) for k in chunks(False, 3 * DS, 4 * DS) for n in tiles(k)]
        + [(None, 0.5, student_unit), (None, 0.4, student_cross), (None, 0.2, student_gram)]
        + [(k, 0.4, bind(features, k, n)) for k in chunks(True, 3 * DT, 4 * DT) for n in tiles(k)]
    )
    steps = {1: stage_1, 2: stage_2, 3: stage_3, 4: stage_4, 5: stage_5}
    for stage, index in plan([task[:2] for task in tasks]):
        if stage:
            steps[stage](index)
        else:
            tasks[index][2]()
    scale, square = state["scale"], state["square"]
    row = lax.rsqrt(square / DT + EPS) * DT**-0.5
    along = jnp.broadcast_to(row, (T, 128)).T[0:1, :]
    diff = 8.0 * (gs[...] - gt[...] * row * along)

    eh = diff.astype(BF)
    el = (diff - eh.astype(F32)).astype(BF)
    along_unit = jnp.sum(diff * gs[...], axis=-1, keepdims=True)
    for n in range(0, DS, 256):
        cols = slice(n, n + 256)
        wide = jnp.concatenate([ul_ref[:, cols], uh_ref[:, cols]], axis=0)
        du = mm(eh, uh_ref[:, cols]) + mm(jnp.concatenate([eh, el], axis=1), wide)
        rg[c, :, 3072 + n : 3328 + n] = (scale * (du - along_unit * rs[:, cols])).astype(BF)
    own_out = rg.at[c, :, 3072:4096]
    send(own_out, own_out, x_send.at[2], x_recv.at[2], sibling)

    def where_to(section, group):
        i = group * oc + section * c
        return lax.rem(section * oc + group * c - ma + 4, 4), i

    def transfer(n, direction, slot):
        send(
            gp.at[n], rx.at[direction, slot], p1_send.at[n], p1_recv.at[direction, slot], a_peer(1 + 2 * direction)
        )

    def emit(section, group):
        n = 4 * section + group
        left = lt[section // 3].reshape(512, 512)
        right = rg[:, :, pl.ds(pl.multiple_of(n * 256, 256), 256)].reshape(512, 256)
        gp[n] = mm(left, right).astype(BF)
        rel, i = where_to(section, group)
        upper = lax.div(i, 2)

        @pl.when(rel == 2)
        def _():
            transfer(n, upper, i - 2 * upper)

        @pl.when((rel == 1) & (i >= 2) | (rel == 3) & (i < 2))
        def _():
            transfer(n, lax.div(rel, 2), 2 + i)

    def settle(section, group):
        n = 4 * section + group
        rel, i = where_to(section, group)
        direction = lax.div(rel, 2)

        @pl.when((rel == 1) & (i < 2) | (rel == 3) & (i >= 2))
        def _():
            slot = i - 2 * direction
            wait(rx.at[0, 0], p1_recv.at[direction, slot])
            gp[n] = (gp[n].astype(F32) + rx[direction, slot].astype(F32)).astype(BF)
            transfer(n, direction, 2 + i)

    def own_cols(core, group):
        return rg.at[core, :, lanes(group * 256, 256)], rg.at[core, :, lanes(DS + group * 256, 256)], rg.at[
            core, :, lanes(2 * DS + group * 256, 256)
        ]

    ones = zero_b + 1.0

    def backward(group):
        first = group * 256
        og = rg[c, :, 3072:4096]
        up = mm(og, Ws[group, :, :, 3072:4096].reshape(256, DS), 1, 1)
        up = up * iv[:, lanes(first, 256)]
        rows = up * ms[:, lanes(first, 256)].astype(F32) * -0.125
        for p in range(2):
            at0 = first + 128 * p
            q, k, v = as_[:, lanes(at0)], as_[:, lanes(DS + at0)], as_[:, lanes(2 * DS + at0)]
            u = up[:, 128 * p : 128 * p + 128]
            grads = both(u.astype(BF))
            left = jnp.concatenate([both((u * 0.125).astype(BF)), both(rows[:, 128 * p : 128 * p + 128].astype(BF))], axis=1)
            dp = mm(left, jnp.concatenate([v, ones], axis=1), 1, 1)
            e = ex[2 * group + p]
            sg = (e.astype(F32) * dp).astype(BF)
            wide = jnp.concatenate([sg[:T], sg[T:]], axis=1)
            rg[c, :, lanes(at0)] = mm(wide, both(k)).astype(BF)
            rg[c, :, lanes(DS + at0)] = mm(sg, both(q), 0, 0).astype(BF)
            rg[c, :, lanes(2 * DS + at0)] = mm(e, grads, 0, 0).astype(BF)
        for section, mine in enumerate(own_cols(c, group)):
            send(mine, mine, g_send.at[group, section], g_recv.at[group, section], sibling)

    def terms(group):
        for section, theirs in enumerate(own_cols(oc, group)):
            wait(theirs, g_recv.at[group, section])
            emit(section, group)

    def nth(k):
        return lax.rem(y + 2 + lax.div(k * (k + 1), 2), 4)

    first_group = lax.rem(y + 2, 4)
    backward(first_group)
    wait(lt.at[0, :, :, 0:T], x_recv.at[0])
    wait(lt.at[1, :, :, 0:T], x_recv.at[1])
    wait(rg.at[0, :, 3072:4096], x_recv.at[2])

    def emit_out(k, carry):
        emit(3, nth(k))
        return carry

    lax.fori_loop(0, 4, emit_out, 0)
    terms(first_group)

    def later(k, carry):
        backward(nth(k))
        terms(nth(k))
        return carry

    lax.fori_loop(1, 4, later, 0)

    def settle_group(k, carry):
        for section in (3, 0, 1, 2):
            settle(section, nth(k))
        return carry

    lax.fori_loop(0, 4, settle_group, 0)

    def close(i):
        n = (4 * ma + i) * oc + (4 * i + ma) * c
        wait(rx.at[0, 0], p1_recv.at[0, 2 + i])
        wait(rx.at[0, 0], p1_recv.at[1, 2 + i])
        gp2[i] = (gp[n].astype(F32) + (rx[0, 2 + i].astype(F32) + rx[1, 2 + i].astype(F32))).astype(BF)

    far_b, right_b, left_b = lax.rem(mb + 2, 4), lax.rem(mb + 1, 4), lax.rem(mb + 3, 4)
    upper, lower = slice(0, 256), slice(256, 512)
    close(far_b)
    send(gp2.at[far_b, upper], bl1, p2_send.at[0], ql1_recv, b_peer(1))
    send(gp2.at[far_b, lower], br1, p2_send.at[1], qr1_recv, b_peer(3))
    close(right_b)
    send(gp2.at[right_b, lower], bl2.at[lower], p2_send.at[2], ql2_recv.at[1], b_peer(1))
    close(left_b)
    send(gp2.at[left_b, upper], br2.at[upper], p2_send.at[3], qr2_recv.at[0], b_peer(3))
    close(mb)
    wait(bl1, ql1_recv)
    gp2[right_b, upper] = (gp2[right_b, upper].astype(F32) + bl1[...].astype(F32)).astype(BF)
    send(gp2.at[right_b, upper], bl2.at[upper], p2_send.at[4], ql2_recv.at[0], b_peer(1))
    wait(br1, qr1_recv)
    gp2[left_b, lower] = (gp2[left_b, lower].astype(F32) + br1[...].astype(F32)).astype(BF)
    send(gp2.at[left_b, lower], br2.at[lower], p2_send.at[5], qr2_recv.at[1], b_peer(3))
    for which in range(2):
        wait(bl1, ql2_recv.at[which])
        wait(bl1, qr2_recv.at[which])
    total = gp2[mb].astype(F32) + (bl2[...].astype(F32) + br2[...].astype(F32))
    z3[...] = total.astype(BF).reshape(8, 64, 256)

    for step in range(1, 8):
        send(z3.at[lax.rem(z + step, 8)], zr.at[step - 1], p3_send.at[step - 1], p3_recv.at[step - 1], z_peer(step))
    acc = z3[z].astype(F32)
    for step in range(1, 8):
        wait(zr.at[0], p3_recv.at[step - 1])
        acc = acc + zr[step - 1].astype(F32)
    out[...] = acc

    for k in range(NC):
        wait(some(k, 2, part(k)), z_send.at[k])
        wait(some(k, 1, part(k)), z2_send.at[k])
        if CHUNKS[k][3]:
            wait(some(k, 6, part(k)), a_send.at[k])
            wait(some(k, 6, part(k, 0)), b_send.at[k])
        wait(core_half(k, 0), c_send.at[k])
    wait(lt.at[0, :, :, 0:T], x_send.at[0])
    wait(lt.at[1, :, :, 0:T], x_send.at[1])
    wait(rg.at[0, :, 3072:4096], x_send.at[2])
    for group in range(4):
        for section, mine in enumerate(own_cols(0, group)):
            wait(mine, g_send.at[group, section])

    def sent(n, carry):
        rel, _ = where_to(lax.div(n, 4), lax.rem(n, 4))

        @pl.when(rel != 0)
        def _():
            wait(rx.at[0, 0], p1_send.at[n])

        return carry

    lax.fori_loop(0, 16, sent, 0)
    for which in range(6):
        wait(bl1, p2_send.at[which])
    for step in range(7):
        wait(zr.at[0], p3_send.at[step])


def per_device(teacher_tokens, teacher_qkv, teacher_out, student_tokens, student_weights):
    vmem = pltpu.VMEM
    dma = pltpu.SemaphoreType.DMA
    any_spec = pl.BlockSpec(memory_space=pl.ANY)
    return pl.pallas_call(
        kernel,
        out_shape=jax.ShapeDtypeStruct((64, 256), F32),
        in_specs=[any_spec] * 5,
        out_specs=pl.BlockSpec(memory_space=pltpu.VMEM),
        scratch_shapes=[
            vmem((4, 2, RT, TW), BF),
            vmem((4, 2, RS, SW), BF),
            vmem((T, DT), BF),
            vmem((T, DS), BF),
            vmem((T, DT), BF),
            vmem((T, DS), BF),
            vmem((T, 3 * DT), BF),
            vmem((T, DT), BF),
            vmem((T, 3 * DS), BF),
            vmem((8, 2 * T, T), BF),
            vmem((T, DS), F32),
            vmem((T, DS), BF),
            vmem((T, DS), F32),
            vmem((T, DS), BF),
            vmem((T, DS), BF),
            vmem((T, T), F32),
            vmem((T, T), F32),
            vmem((2, 8, 2, 64, T), BF),
            vmem((2, 8, 64, 2 * T), BF),
            vmem((2, T, SW), BF),
            vmem((16, 512, 256), BF),
            vmem((2, 6, 512, 256), BF),
            vmem((4, 512, 256), BF),
            vmem((256, 256), BF),
            vmem((256, 256), BF),
            vmem((512, 256), BF),
            vmem((512, 256), BF),
            vmem((8, 64, 256), BF),
            vmem((7, 64, 256), BF),
            dma((5,)),
            dma((NC,)), dma((NC,)), dma((NC,)), dma((NC,)), dma((NC,)), dma((NC,)),
            dma((NC,)), dma((NC,)), dma((NC,)),
            dma((NC,)), dma((NC,)), dma((NC,)),
            dma((NC,)), dma((NC,)),
            dma((3,)), dma((3,)),
            dma((4, 3)), dma((4, 3)),
            dma((16,)), dma((2, 6)),
            dma((6,)), dma, dma, dma((2,)), dma((2,)),
            dma((7,)), dma((7,)),
        ],
        compiler_params=pltpu.CompilerParams(
            collective_id=0, has_side_effects=True, vmem_limit_bytes=62 * 1024 * 1024
        ),
        cost_estimate=pl.CostEstimate(flops=11_400_000_000, bytes_accessed=30_000_000, transcendentals=2_700_000),
        name="distill",
    )(teacher_tokens, teacher_qkv, teacher_out, student_tokens, student_weights)


def solution(mesh):
    return jax.shard_map(
        per_device,
        mesh=mesh,
        in_specs=(
            P(("rows", "dp"), None),
            P("rows", None),
            P("rows", None),
            P(("rows", "dp"), None),
            P("rows", None),
        ),
        out_specs=P(("group", "rows"), "dp"),
        check_vma=False,
    )
```
